128 devices in a mesh: row: 8 (over x, core), col: 16 (over y, z).
Axes of the slice: x: 4, y: 4, z: 4, core: 2. Of those that a mesh axis runs over, the one named last changes fastest.
Arguments:
- eta_pairs: bfloat16 [12288, 12288], P('row', 'col'), may hold values from -6 to 6
- gamma_pairs: bfloat16 [12288, 12288], P('row', 'col'), may hold values from -0.0546875 to 0.0546875
- pair_first: int32 [12288], P('row'), may hold values from 0 to 239
- pair_second: int32 [12288], P('row'), may hold values from 0 to 239
- occupancy: float32 [240], replicated, may hold values from 0 to 1
- gamma_recoupled: bfloat16 [128, 1536, 1536], P(('row', 'col')), may hold values from -0.15625 to 0.15625
- ph_factor: float32 [128, 1536], P(('row', 'col')), may hold values from -1 to 1
- tile_source: int32 [128, 144], P(('row', 'col')), may hold values from 0 to 71, as said below
- tile_owner: int32 [128, 144], P(('row', 'col')), may hold values from 0 to 127, as said below
- tile_place: int32 [128, 144], P(('row', 'col')), may hold values from 0 to 143
- sixj_weight: bfloat16 [128, 144], P(('row', 'col')), may hold values from -1 to 1
- live_count: int32 [128], P(('row', 'col')), may hold values from 72 to 144, as said below
Outputs:
- panel_update: bfloat16 [2048, 12288], P('col', 'row')
- recoupled_update: bfloat16 [12288, 12288], P('row', 'col')
The draws below stay inside these ranges and needn't reach their ends.
Inputs may be any that keep to these rules, and one draw needn't show every extreme that they name: `tile_source`: in each row the first 72 entries name every tile of the block once. `tile_owner`: in each row no channel is named by more than 2 entries; one channel is named exactly 2 times within the first 72 entries of every row. `live_count`: some block has 144 live slots and another 72.
All inputs are finite; a program needn't handle non-finite values.
Results may differ from the reference program's by a relative error of at most 0.019.
Values may be sent and summed in bfloat16 or wider, within the bound.
No kernel may reach another device: no remote copies, remote signals or barrier semaphores. Data moves between devices by JAX's collectives and lax.ppermute only.
A program may use at most 128 MiB of HBM per device.

```python
import jax
import jax.numpy as jnp
from jax import lax

TILE = 128
PAIRS = 12288
ORBITS = 240
PH_STATES = 1536
PANEL_DEV = 128
BLOCK_ROWS = 1536
BLOCK_COLS = 768
PANEL = 2048
BLOCKS = 128
TILES_BLOCK = 72
SLOTS = 144
CAP = 2
PH_TILES = 12
N_ROW = 8
N_COL = 16


def draw_tile_source(key, part):
    key = jax.random.fold_in(key, 11)
    cover_key, extra_key = jax.random.split(key)

    def one_row(row_key):
        return jax.random.permutation(row_key, TILES_BLOCK).astype(jnp.int32)
    covering = jax.vmap(one_row)(jax.random.split(cover_key, BLOCKS))
    extra = jax.random.randint(extra_key, (BLOCKS, SLOTS - TILES_BLOCK), 0, TILES_BLOCK).astype(jnp.int32)
    return jnp.concatenate([covering, extra], axis=1)


def draw_tile_owner(key, part):
    key = jax.random.fold_in(key, 23)
    busy_key, rows_key = jax.random.split(key)
    busiest = jax.random.randint(busy_key, (), 0, BLOCKS).astype(jnp.int32)
    spare_ids = jnp.arange((BLOCKS - 1) * CAP, dtype=jnp.int32) // CAP
    spare_ids = spare_ids + (spare_ids >= busiest).astype(jnp.int32)

    def one_row(row_key):
        sub_keys = jax.random.split(row_key, 3)
        shuffled = jax.random.permutation(sub_keys[0], spare_ids)[:SLOTS - CAP]
        row_owners = jnp.concatenate([jnp.full((CAP,), busiest, jnp.int32), shuffled])
        leading = jax.random.permutation(sub_keys[1], row_owners[:TILES_BLOCK])
        trailing = jax.random.permutation(sub_keys[2], row_owners[TILES_BLOCK:])
        return jnp.concatenate([leading, trailing]).astype(jnp.int32)
    return jax.vmap(one_row)(jax.random.split(rows_key, BLOCKS))


def draw_live_count(key, part):
    key = jax.random.fold_in(key, 37)
    sub_keys = jax.random.split(key, 3)
    counts = jax.random.randint(sub_keys[0], (BLOCKS,), TILES_BLOCK, SLOTS + 1).astype(jnp.int32)
    full_row = jax.random.randint(sub_keys[1], (), 0, BLOCKS)
    least_row = (full_row + 1 + jax.random.randint(sub_keys[2], (), 0, BLOCKS - 1)) % BLOCKS
    return counts.at[full_row].set(SLOTS).at[least_row].set(TILES_BLOCK).astype(jnp.int32)


def with_ends(result, rng, low, top_value):
    spot = [jax.random.randint(jax.random.fold_in(rng, axis), (), 0, length) for axis, length in enumerate(result.shape)]
    longest = result.shape.index(max(result.shape))
    neighbour = spot[:longest] + [(spot[longest] + 1) % result.shape[longest]] + spot[longest + 1:]
    return result.at[tuple(spot)].set(low).at[tuple(neighbour)].set(top_value)


def levels(stream_key, shape, cuts, smallest, high):
    def one(axis_at, blocks):
        heights = jax.random.uniform(jax.random.fold_in(jax.random.fold_in(stream_key, 6), axis_at), (blocks,), jnp.float32, smallest / len(cuts), high / len(cuts))
        return jnp.repeat(jnp.exp(heights), shape[axis_at] // blocks).reshape((-1,) + (1,) * (len(shape) - axis_at - 1))

    loudness = one(*cuts[0])
    for cut in cuts[1:]:
        loudness = loudness * one(*cut)
    return loudness


def noise(rng, dims, scale, most, pieces=(), held_as=jnp.bfloat16):
    level = levels(rng, dims, pieces, -0.22, 0.18) if pieces else 1.0
    result = jax.random.normal(rng, dims, jnp.float32) * scale * level
    return jnp.minimum(jnp.maximum(result, -most), most).astype(held_as)


def setup_inputs(seed: int = 0) -> dict:
    splits = jax.random.split(jax.random.key(seed), 13)
    return {
        "eta_pairs": noise(splits[0], (PAIRS, PAIRS), 1.0, 6.0, ((0, 8), (1, 16))),
        "gamma_pairs": noise(splits[1], (PAIRS, PAIRS), PAIRS ** -0.5, 0.0546875, ((0, 8), (1, 16))),
        "pair_first": with_ends(jax.random.randint(splits[2], (PAIRS,), 0, ORBITS), jax.random.fold_in(splits[2], 1), 0, ORBITS - 1).astype(jnp.int32),
        "pair_second": with_ends(jax.random.randint(splits[3], (PAIRS,), 0, ORBITS), jax.random.fold_in(splits[3], 1), 0, ORBITS - 1).astype(jnp.int32),
        "occupancy": jnp.clip(jax.random.uniform(splits[4], (ORBITS,), jnp.float32, 0.0, 1.0), 0.0, 1.0),
        "gamma_recoupled": noise(splits[5], (BLOCKS, PH_STATES, PH_STATES), PH_STATES ** -0.5, 0.15625, ((0, 128),)),
        "ph_factor": jnp.clip(jax.random.uniform(splits[6], (BLOCKS, PH_STATES), jnp.float32, -1.0, 1.0) * levels(splits[6], (BLOCKS, PH_STATES), ((0, 128),), -0.4, 0.0), -1.0, 1.0),
        "tile_source": draw_tile_source(jax.random.fold_in(splits[12], 71), 0),
        "tile_owner": draw_tile_owner(jax.random.fold_in(splits[12], 71), 0),
        "tile_place": with_ends(jax.random.randint(splits[9], (BLOCKS, SLOTS), 0, PH_TILES * PH_TILES), jax.random.fold_in(splits[9], 1), 0, (PH_TILES * PH_TILES) - 1).astype(jnp.int32),
        "sixj_weight": jnp.clip(jax.random.uniform(splits[10], (BLOCKS, SLOTS), jnp.float32, -1.0, 1.0) * levels(splits[10], (BLOCKS, SLOTS), ((0, 128),), -0.4, 0.0), -1.0, 1.0).astype(jnp.bfloat16),
        "live_count": draw_live_count(jax.random.fold_in(splits[12], 71), 0),
    }


def orbit_lookup(pair_ids, occupancy):
    orbit_ids = jnp.arange(ORBITS, dtype=jnp.int32)
    return jnp.sum(jnp.where(pair_ids[:, None] == orbit_ids[None, :], occupancy[None, :], 0.0), axis=1)


def reference(eta_pairs, gamma_pairs, pair_first, pair_second, occupancy, gamma_recoupled, ph_factor, tile_source, tile_owner, tile_place, sixj_weight, live_count):
    factor = 1.0 - orbit_lookup(pair_first, occupancy) - orbit_lookup(pair_second, occupancy)
    panel_ids = jnp.arange(PANEL, dtype=jnp.int32)
    columns = (panel_ids // PANEL_DEV) * BLOCK_COLS + panel_ids % PANEL_DEV
    gamma_panel = (factor[:, None] * gamma_pairs[:, columns].astype(jnp.float32)).astype(jnp.bfloat16)
    eta_panel = (factor[:, None] * eta_pairs[:, columns].astype(jnp.float32)).astype(jnp.bfloat16)
    panel_total = jnp.zeros((PANEL, PAIRS), jnp.float32)
    for column_block in range(N_COL):
        lower = column_block * BLOCK_COLS
        upper = lower + BLOCK_COLS
        block_sum = jnp.dot(eta_pairs[:, lower:upper], gamma_panel[lower:upper], preferred_element_type=jnp.float32)
        block_sum = block_sum - jnp.dot(gamma_pairs[:, lower:upper], eta_panel[lower:upper], preferred_element_type=jnp.float32)
        rounded = lax.optimization_barrier(block_sum.astype(jnp.bfloat16))
        panel_total = panel_total + rounded.T.astype(jnp.float32)
    panel_update = panel_total.astype(jnp.bfloat16)

    row_tiles = BLOCK_ROWS // TILE
    col_tiles = BLOCK_COLS // TILE
    eta_tiles = eta_pairs.reshape(N_ROW, row_tiles, TILE, N_COL, col_tiles, TILE)
    eta_tiles = eta_tiles.transpose(0, 3, 1, 4, 2, 5).reshape(BLOCKS, TILES_BLOCK, TILE, TILE)
    slot_ids = jnp.arange(SLOTS, dtype=jnp.int32)

    def add_block(accumulated, inputs):
        block_tiles, sources, owners, places, weights, live = inputs
        picked = block_tiles[sources]
        sent = (weights.astype(jnp.float32)[:, None, None] * picked.astype(jnp.float32)).astype(jnp.bfloat16)
        sent = lax.optimization_barrier(sent)
        is_live = slot_ids < live
        contrib = jnp.where(is_live[:, None, None], sent.astype(jnp.float32), 0.0)
        return accumulated.at[owners, places].add(contrib), None

    start_sums = jnp.zeros((BLOCKS, PH_TILES * PH_TILES, TILE, TILE), jnp.float32)
    accumulated, _ = lax.scan(add_block, start_sums, (eta_tiles, tile_source, tile_owner, tile_place, sixj_weight, live_count))
    eta_recoupled = accumulated.reshape(BLOCKS, PH_TILES, PH_TILES, TILE, TILE).transpose(0, 1, 3, 2, 4)
    eta_recoupled = eta_recoupled.reshape(BLOCKS, PH_STATES, PH_STATES).astype(jnp.bfloat16)

    def one_channel(inputs):
        eta_ph, gamma_ph, scale = inputs
        gamma_scaled = (scale[:, None] * gamma_ph.astype(jnp.float32)).astype(jnp.bfloat16)
        eta_scaled = (scale[:, None] * eta_ph.astype(jnp.float32)).astype(jnp.bfloat16)
        product = jnp.dot(eta_ph, gamma_scaled, preferred_element_type=jnp.float32)
        product = product - jnp.dot(gamma_ph, eta_scaled, preferred_element_type=jnp.float32)
        return product.astype(jnp.bfloat16)

    ph_product = lax.map(one_channel, (eta_recoupled, gamma_recoupled, ph_factor))
    product_tiles = ph_product.reshape(BLOCKS, PH_TILES, TILE, PH_TILES, TILE).transpose(0, 1, 3, 2, 4)
    product_tiles = product_tiles.reshape(BLOCKS, PH_TILES * PH_TILES, TILE, TILE)

    def back_block(inputs):
        sources, owners, places, weights, live = inputs
        picked = product_tiles[owners, places]
        is_live = slot_ids < live
        contrib = jnp.where(is_live[:, None, None], weights.astype(jnp.float32)[:, None, None] * picked.astype(jnp.float32), 0.0)
        gathered = jnp.zeros((TILES_BLOCK, TILE, TILE), jnp.float32).at[sources].add(contrib)
        return gathered.astype(jnp.bfloat16)

    updates = lax.map(back_block, (tile_source, tile_owner, tile_place, sixj_weight, live_count))
    updates = updates.reshape(N_ROW, N_COL, row_tiles, col_tiles, TILE, TILE).transpose(0, 2, 4, 1, 3, 5)
    recoupled_update = updates.reshape(PAIRS, PAIRS)
    return panel_update, recoupled_update
```

```python
import jax
import jax.numpy as jnp
from jax import lax
from jax.experimental import pallas as pl
from jax.experimental.pallas import tpu as pltpu
from jax.sharding import PartitionSpec as P

TILE = 128
ORBITS = 240
PH_STATES = 1536
PH_TILES = 12
PANEL_DEV = 128
ROWS = 1536
COLS = 768
COL_TILES = 6
TILES_BLOCK = 72
SLOTS = 144
BLOCKS = 128
CAP = 2
N_ROW = 8
N_COL = 16
VMEM_LIMIT = 60 * 1024 * 1024

f32 = jnp.float32
bf16 = jnp.bfloat16
SMEM = pltpu.MemorySpace.SMEM
VMEM = pltpu.MemorySpace.VMEM


def smem_spec():
    return pl.BlockSpec(memory_space=SMEM)


def vmem_spec():
    return pl.BlockSpec(memory_space=VMEM)


def params():
    return pltpu.CompilerParams(vmem_limit_bytes=VMEM_LIMIT)


def aligned(start, size):
    return pl.ds(pl.multiple_of(start * size, size), size)


def clear_counts(counts):
    def step(q, carry):
        counts[q] = 0
        return carry

    lax.fori_loop(0, BLOCKS, step, 0)


def buffer_slot(owner_ref, counts, s):
    q = owner_ref[0, s]
    k = counts[q]
    counts[q] = k + 1
    return q * CAP + k


def block_tile(source_ref, s):
    t = source_ref[0, s]
    r = t // COL_TILES
    return aligned(r, TILE), aligned(t - r * COL_TILES, TILE)


def send_kernel(live_ref, source_ref, owner_ref, weight_ref, eta_ref, out_ref, counts):
    clear_counts(counts)

    def step(s, carry):
        n = buffer_slot(owner_ref, counts, s)
        rows, cols = block_tile(source_ref, s)
        out_ref[n] = (weight_ref[0, s] * eta_ref[rows, cols].astype(f32)).astype(bf16)
        return carry

    lax.fori_loop(0, live_ref[0], step, 0)


def update_kernel(live_ref, source_ref, owner_ref, weight_ref, back_ref, out_ref, counts, total):
    clear_counts(counts)

    def first(s, carry):
        n = buffer_slot(owner_ref, counts, s)
        rows, cols = block_tile(source_ref, s)
        total[rows, cols] = weight_ref[0, s] * back_ref[n].astype(f32)
        return carry

    def later(s, carry):
        n = buffer_slot(owner_ref, counts, s)
        rows, cols = block_tile(source_ref, s)
        total[rows, cols] += weight_ref[0, s] * back_ref[n].astype(f32)
        return carry

    lax.fori_loop(0, TILES_BLOCK, first, 0)
    lax.fori_loop(TILES_BLOCK, live_ref[0], later, 0)

    def finish(r, carry):
        rows = aligned(r, TILE)
        out_ref[rows, :] = total[rows, :].astype(bf16)
        return carry

    lax.fori_loop(0, ROWS // TILE, finish, 0)


def channel_kernel(
    code_ref, got_ref, gamma_ref, scale_ref, out_ref, total, eta, eta_scaled, gamma_scaled, product
):
    def clear(r, carry):
        total[aligned(r, TILE), :] = jnp.zeros((TILE, PH_STATES), f32)
        return carry

    lax.fori_loop(0, PH_TILES, clear, 0)

    def place_of(code):
        r = code // PH_TILES
        return aligned(r, TILE), aligned(code - r * PH_TILES, TILE)

    def add(n, carry):
        code = code_ref[n]

        @pl.when(code >= 0)
        def _():
            rows, cols = place_of(code)
            total[rows, cols] += got_ref[n].astype(f32)

        return carry

    lax.fori_loop(0, BLOCKS * CAP, add, 0)

    def scale_rows(r, carry):
        rows = aligned(r, TILE)
        scale = scale_ref[rows, :]
        whole = total[rows, :].astype(bf16)
        eta[rows, :] = whole
        eta_scaled[rows, :] = (-scale * whole.astype(f32)).astype(bf16)
        gamma_scaled[rows, :] = (scale * gamma_ref[rows, :].astype(f32)).astype(bf16)
        return carry

    lax.fori_loop(0, PH_TILES, scale_rows, 0)

    width = 256

    def multiply(c, carry):
        cols = aligned(c, width)
        part = jnp.dot(eta[...], gamma_scaled[:, cols], preferred_element_type=f32)
        part += jnp.dot(gamma_ref[...], eta_scaled[:, cols], preferred_element_type=f32)
        product[:, cols] = part.astype(bf16)
        return carry

    lax.fori_loop(0, PH_STATES // width, multiply, 0)

    def answer(n, carry):
        code = code_ref[n]

        @pl.when(code >= 0)
        def _():
            rows, cols = place_of(code)
            out_ref[n] = product[rows, cols]

        return carry

    lax.fori_loop(0, BLOCKS * CAP, answer, 0)


def panel_kernel(eta_ref, gamma_ref, panel_ref, out_ref):
    gamma_cols = jnp.concatenate([panel_ref[0, 0], panel_ref[1, 0]], axis=1)
    eta_cols = jnp.concatenate([panel_ref[0, 1], panel_ref[1, 1]], axis=1)
    part = jnp.dot(eta_ref[...], gamma_cols, preferred_element_type=f32)
    part -= jnp.dot(gamma_ref[...], eta_cols, preferred_element_type=f32)
    part = part.astype(bf16)
    for k in range(2):
        out_ref[k] = part[:, k * PANEL_DEV : (k + 1) * PANEL_DEV]


def turn_kernel(in_ref, out_ref):
    out_ref[...] = in_ref[...].astype(f32).T.astype(bf16)


def orbit_lookup(pair_ids, occupancy):
    orbit_ids = jnp.arange(occupancy.shape[0], dtype=jnp.int32)
    return jnp.sum(
        jnp.where(pair_ids[:, None] == orbit_ids[None, :], occupancy[None, :], 0.0), axis=1
    )


def panel_part(eta_pairs, gamma_pairs, pair_first, pair_second, occupancy, codes):
    factor = 1.0 - orbit_lookup(pair_first, occupancy) - orbit_lookup(pair_second, occupancy)

    def weigh(pairs):
        return (factor[:, None] * pairs[:, :PANEL_DEV].astype(f32)).astype(bf16)

    halves = jnp.stack([weigh(gamma_pairs), weigh(eta_pairs)]).reshape(2, 2, COLS, PANEL_DEV)
    odd = lax.axis_index("col") % 2 == 1

    def swap(first, second):
        return jnp.where(odd, second, first), jnp.where(odd, first, second)

    def route(flip):
        return [
            (i * N_COL + c, (c // 2) * N_COL + 2 * i + (c + flip) % 2)
            for i in range(N_ROW)
            for c in range(N_COL)
        ]

    same, other = swap(halves[:, 0], halves[:, 1])
    same = lax.ppermute(same, ("row", "col"), route(0))
    other = lax.ppermute(other, ("row", "col"), route(1))
    pieces = jnp.stack(swap(same, other))
    whole = lax.all_gather(
        pieces.reshape(4 * COLS, PANEL_DEV), "row", axis=0, tiled=True
    ).reshape(N_COL, 2, COLS, PANEL_DEV)
    whole, codes = lax.optimization_barrier((whole, codes))
    sums = pl.pallas_call(
        panel_kernel,
        grid=(N_COL // 2,),
        in_specs=[
            pl.BlockSpec((ROWS, COLS), lambda c: (0, 0)),
            pl.BlockSpec((ROWS, COLS), lambda c: (0, 0)),
            pl.BlockSpec((2, 2, COLS, PANEL_DEV), lambda c: (c, 0, 0, 0)),
        ],
        out_specs=pl.BlockSpec((2, ROWS, PANEL_DEV), lambda c: (c, 0, 0)),
        out_shape=jax.ShapeDtypeStruct((N_COL, ROWS, PANEL_DEV), bf16),
        compiler_params=params(),
        cost_estimate=pl.CostEstimate(
            flops=4 * ROWS * COLS * N_COL * PANEL_DEV, bytes_accessed=20 << 20, transcendentals=0
        ),
        name="panel",
    )(eta_pairs, gamma_pairs, whole)
    sums, codes = lax.optimization_barrier((sums, codes))
    done = lax.psum_scatter(
        sums.reshape(N_COL * ROWS, PANEL_DEV), "col", scatter_dimension=0, tiled=True
    )
    return pl.pallas_call(
        turn_kernel,
        in_specs=[vmem_spec()],
        out_specs=vmem_spec(),
        out_shape=jax.ShapeDtypeStruct((PANEL_DEV, ROWS), bf16),
        compiler_params=params(),
        name="turn",
    )(done), codes


def received_codes(owners, places, live):
    slot_ids = jnp.arange(SLOTS, dtype=jnp.int32)
    packed = jnp.where(slot_ids[None, :] < live, owners * 256 + places, -1)
    table = packed
    for axis, size in (("col", N_COL), ("row", N_ROW)):
        place = lax.axis_index(axis)
        span = 1
        while span < size:
            pairs = [(d, d ^ span) for d in range(size)]
            theirs = lax.ppermute(table, axis, pairs)
            upper = (place // span) % 2 == 1
            table = jnp.concatenate(
                [jnp.where(upper, theirs, table), jnp.where(upper, table, theirs)]
            )
            span *= 2
    me = lax.axis_index("row") * N_COL + lax.axis_index("col")
    none = jnp.int32(1 << 20)
    keys = jnp.where((table >> 8) == me, slot_ids[None, :] * 256 + (table & 255), none)
    first = jnp.min(keys, axis=1, keepdims=True)
    second = jnp.min(jnp.where(keys > first, keys, none), axis=1, keepdims=True)
    both = jnp.concatenate([first, second], axis=1)
    return jnp.where(both < none, both & 255, -1).reshape(BLOCKS * CAP)


def exchange(tiles):
    shape = (BLOCKS, CAP * TILE, TILE)
    moved = lax.all_to_all(
        tiles.reshape(shape), ("row", "col"), split_axis=0, concat_axis=0, tiled=True
    )
    return moved.reshape(BLOCKS * CAP, TILE, TILE)


def recoupled_part(
    eta_pairs,
    gamma_recoupled,
    ph_factor,
    tile_source,
    tile_owner,
    tile_place,
    sixj_weight,
    live_count,
    codes,
):
    weights = sixj_weight.astype(f32)
    slots_shape = jax.ShapeDtypeStruct((BLOCKS * CAP, TILE, TILE), bf16)
    counts = pltpu.SMEM((BLOCKS,), jnp.int32)
    sent = pl.pallas_call(
        send_kernel,
        in_specs=[smem_spec()] * 4 + [vmem_spec()],
        out_specs=vmem_spec(),
        out_shape=slots_shape,
        scratch_shapes=[counts],
        compiler_params=params(),
        cost_estimate=pl.CostEstimate(flops=0, bytes_accessed=11 << 20, transcendentals=0),
        name="send",
    )(live_count, tile_source, tile_owner, weights, eta_pairs)
    received = exchange(sent)
    whole = (PH_STATES, PH_STATES)
    answers = pl.pallas_call(
        channel_kernel,
        in_specs=[smem_spec()] + [vmem_spec()] * 3,
        out_specs=vmem_spec(),
        out_shape=slots_shape,
        scratch_shapes=[pltpu.VMEM(whole, f32)] + [pltpu.VMEM(whole, bf16)] * 4,
        compiler_params=params(),
        cost_estimate=pl.CostEstimate(
            flops=4 * PH_STATES**3, bytes_accessed=22 << 20, transcendentals=0
        ),
        name="channel",
    )(codes, received, gamma_recoupled[0], ph_factor.reshape(PH_STATES, 1))
    returned = exchange(answers)
    return pl.pallas_call(
        update_kernel,
        in_specs=[smem_spec()] * 4 + [vmem_spec()],
        out_specs=vmem_spec(),
        out_shape=jax.ShapeDtypeStruct((ROWS, COLS), bf16),
        scratch_shapes=[counts, pltpu.VMEM((ROWS, COLS), f32)],
        compiler_params=params(),
        cost_estimate=pl.CostEstimate(flops=0, bytes_accessed=11 << 20, transcendentals=0),
        name="update",
    )(live_count, tile_source, tile_owner, weights, returned)


def local(
    eta_pairs,
    gamma_pairs,
    pair_first,
    pair_second,
    occupancy,
    gamma_recoupled,
    ph_factor,
    tile_source,
    tile_owner,
    tile_place,
    sixj_weight,
    live_count,
):
    codes = received_codes(tile_owner, tile_place, live_count[0])
    panel_update, codes = panel_part(
        eta_pairs, gamma_pairs, pair_first, pair_second, occupancy, codes
    )
    recoupled_update = recoupled_part(
        eta_pairs,
        gamma_recoupled,
        ph_factor,
        tile_source,
        tile_owner,
        tile_place,
        sixj_weight,
        live_count,
        codes,
    )
    return (panel_update, recoupled_update)


def solution(mesh):
    in_specs = (
        P("row", "col"),
        P("row", "col"),
        P("row"),
        P("row"),
        P(),
        P(("row", "col"), None, None),
        P(("row", "col"), None),
        P(("row", "col"), None),
        P(("row", "col"), None),
        P(("row", "col"), None),
        P(("row", "col"), None),
        P(("row", "col")),
    )
    out_specs = (P("col", "row"), P("row", "col"))
    return jax.shard_map(local, mesh=mesh, in_specs=in_specs, out_specs=out_specs, check_vma=False)
```

```python
import jax
import jax.numpy as jnp
from jax import lax
from jax.experimental import pallas as pl
from jax.experimental.pallas import tpu as pltpu
from jax.sharding import PartitionSpec as P

TILE = 128
ORBITS = 240
PH_STATES = 1536
PH_TILES = 12
PANEL_DEV = 128
ROWS = 1536
COLS = 768
COL_TILES = 6
TILES_BLOCK = 72
SLOTS = 144
BLOCKS = 128
CAP = 2
N_ROW = 8
N_COL = 16
GROUP = 16
CODE_ROWS = 8
VMEM_LIMIT = 60 * 1024 * 1024

f32 = jnp.float32
bf16 = jnp.bfloat16
SMEM = pltpu.MemorySpace.SMEM
VMEM = pltpu.MemorySpace.VMEM


def smem_spec():
    return pl.BlockSpec(memory_space=SMEM)


def any_spec():
    return pl.BlockSpec(memory_space=pl.ANY)


def vmem_spec():
    return pl.BlockSpec(memory_space=VMEM)


def params():
    return pltpu.CompilerParams(vmem_limit_bytes=VMEM_LIMIT)


def aligned(start, size):
    return pl.ds(pl.multiple_of(start * size, size), size)


def step_through(count, unroll, body):
    def step(i, carry):
        for j in range(unroll):
            body(i * unroll + j)
        return carry

    lax.fori_loop(0, count // unroll, step, 0)


def send_kernel(
    live_ref,
    source_ref,
    owner_ref,
    place_ref,
    weight_ref,
    eta_ref,
    out_ref,
    tile_ref,
    factor_ref,
    place_of,
    counts,
    held,
    sems,
):
    def clear(n):
        tile_ref[n] = 0
        factor_ref[n] = 0.0
        place_of[n] = 0

    step_through(BLOCKS * CAP, 8, clear)

    def clear_count(q):
        counts[q] = 0

    step_through(BLOCKS, 8, clear_count)

    def slot(s, carry):
        q = owner_ref[0, s]
        k = counts[q]
        counts[q] = k + 1
        n = q * CAP + k
        t = source_ref[0, s]
        r = t // COL_TILES
        tile_ref[n] = r * 8 + (t - r * COL_TILES)
        factor_ref[n] = weight_ref[0, s]
        place_of[n] = place_ref[0, s]
        return carry

    lax.fori_loop(0, live_ref[0], slot, 0)
    lane = lax.broadcasted_iota(jnp.int32, (CODE_ROWS, TILE), 1)

    def copy(j):
        part = pl.ds(j * GROUP, GROUP)
        return pltpu.make_async_copy(held.at[part], out_ref.at[part], sems.at[j])

    def group(j, carry):
        def owner(i):
            q = j * GROUP + i
            for k in range(CAP):
                n = q * CAP + k
                t = tile_ref[n]
                tile = eta_ref[aligned(t >> 3, TILE), aligned(t & 7, TILE)]
                held[q, k * TILE : (k + 1) * TILE, :] = (
                    factor_ref[n] * tile.astype(f32)
                ).astype(bf16)
            codes = jnp.where(lane == 0, place_of[q * CAP], place_of[q * CAP + 1])
            held[q, CAP * TILE : CAP * TILE + CODE_ROWS, :] = codes.astype(f32).astype(bf16)

        step_through(GROUP, 4, owner)
        copy(j).start()
        return carry

    lax.fori_loop(0, BLOCKS // GROUP, group, 0)

    def finish(j):
        copy(j).wait()

    step_through(BLOCKS // GROUP, 1, finish)


def update_kernel(tile_ref, factor_ref, back_ref, out_ref, held, total, sems):
    def copy(j):
        part = pl.ds(j * GROUP, GROUP)
        return pltpu.make_async_copy(back_ref.at[part], held.at[part], sems.at[j])

    def begin(j):
        copy(j).start()

    step_through(BLOCKS // GROUP, 1, begin)

    def clear(r):
        total[aligned(r, TILE), :] = jnp.zeros((TILE, COLS), f32)

    step_through(ROWS // TILE, 1, clear)

    def group(j, carry):
        copy(j).wait()

        def owner(i):
            q = j * GROUP + i
            for k in range(CAP):
                n = q * CAP + k
                t = tile_ref[n]
                rows, cols = aligned(t >> 3, TILE), aligned(t & 7, TILE)
                total[rows, cols] += factor_ref[n] * held[
                    q, k * TILE : (k + 1) * TILE, :
                ].astype(f32)

        step_through(GROUP, 4, owner)
        return carry

    lax.fori_loop(0, BLOCKS // GROUP, group, 0)

    def finish(r):
        rows = aligned(r, TILE)
        out_ref[rows, :] = total[rows, :].astype(bf16)

    step_through(ROWS // TILE, 1, finish)


def channel_kernel(
    place_ref,
    got_ref,
    gamma_hbm,
    scale_ref,
    out_ref,
    held,
    gamma_ref,
    total,
    eta,
    product,
    got_sems,
    gamma_sem,
    out_sems,
):
    def copy(j):
        part = pl.ds(j * GROUP, GROUP)
        return pltpu.make_async_copy(
            got_ref.at[part, pl.ds(0, CAP * TILE)], held.at[part], got_sems.at[j]
        )

    gamma_copy = pltpu.make_async_copy(gamma_hbm, gamma_ref, gamma_sem)

    def begin(j):
        copy(j).start()

    step_through(BLOCKS // GROUP, 1, begin)
    gamma_copy.start()

    def clear(r):
        total[aligned(r, TILE), :] = jnp.zeros((TILE, PH_STATES), f32)

    step_through(PH_TILES, 1, clear)

    def place(n):
        code = place_ref[n]
        return aligned(code >> 4, TILE), aligned(code & 15, TILE)

    def group(j, carry):
        copy(j).wait()

        def block(i):
            b = j * GROUP + i
            for k in range(CAP):
                rows, cols = place(b * CAP + k)
                total[rows, cols] += held[b, k * TILE : (k + 1) * TILE, :].astype(f32)

        step_through(GROUP, 4, block)
        return carry

    lax.fori_loop(0, BLOCKS // GROUP, group, 0)

    def settle(r):
        rows = aligned(r, TILE)
        eta[rows, :] = total[rows, :].astype(bf16)

    step_through(PH_TILES, 1, settle)
    gamma_copy.wait()
    width = 256

    def multiply(c):
        cols = aligned(c, width)
        scale = scale_ref[...]
        gamma_scaled = (scale * gamma_ref[:, cols].astype(f32)).astype(bf16)
        eta_scaled = (-scale * eta[:, cols].astype(f32)).astype(bf16)
        part = jnp.dot(eta[...], gamma_scaled, preferred_element_type=f32)
        part += jnp.dot(gamma_ref[...], eta_scaled, preferred_element_type=f32)
        product[:, cols] = part.astype(bf16)

    step_through(PH_STATES // width, 1, multiply)

    def back(j):
        part = pl.ds(j * GROUP, GROUP)
        return pltpu.make_async_copy(held.at[part], out_ref.at[part], out_sems.at[j])

    def answers(j, carry):
        def block(i):
            b = j * GROUP + i
            for k in range(CAP):
                rows, cols = place(b * CAP + k)
                held[b, k * TILE : (k + 1) * TILE, :] = product[rows, cols]

        step_through(GROUP, 4, block)
        back(j).start()
        return carry

    lax.fori_loop(0, BLOCKS // GROUP, answers, 0)

    def finish(j):
        back(j).wait()

    step_through(BLOCKS // GROUP, 1, finish)


def panel_kernel(eta_ref, gamma_ref, panel_ref, out_ref):
    gamma_cols = jnp.concatenate([panel_ref[0, 0], panel_ref[1, 0]], axis=1)
    eta_cols = jnp.concatenate([panel_ref[0, 1], panel_ref[1, 1]], axis=1)
    part = jnp.dot(eta_ref[...], gamma_cols, preferred_element_type=f32)
    part -= jnp.dot(gamma_ref[...], eta_cols, preferred_element_type=f32)
    part = part.astype(bf16)
    for k in range(2):
        out_ref[k] = part[:, k * PANEL_DEV : (k + 1) * PANEL_DEV]


def turn_kernel(in_ref, out_ref):
    out_ref[...] = in_ref[...].astype(f32).T.astype(bf16)


def orbit_lookup(pair_ids, occupancy):
    orbit_ids = jnp.arange(occupancy.shape[0], dtype=jnp.int32)
    return jnp.sum(
        jnp.where(pair_ids[:, None] == orbit_ids[None, :], occupancy[None, :], 0.0), axis=1
    )


def panel_pieces(eta_pairs, gamma_pairs, pair_first, pair_second, occupancy):
    factor = 1.0 - orbit_lookup(pair_first, occupancy) - orbit_lookup(pair_second, occupancy)

    def weigh(pairs):
        return (factor[:, None] * pairs[:, :PANEL_DEV].astype(f32)).astype(bf16)

    halves = jnp.stack([weigh(gamma_pairs), weigh(eta_pairs)]).reshape(2, 2, COLS, PANEL_DEV)
    odd = lax.axis_index("col") % 2 == 1

    def swap(first, second):
        return jnp.where(odd, second, first), jnp.where(odd, first, second)

    def route(flip):
        return [
            (i * N_COL + c, (c // 2) * N_COL + 2 * i + (c + flip) % 2)
            for i in range(N_ROW)
            for c in range(N_COL)
        ]

    same, other = swap(halves[:, 0], halves[:, 1])
    same = lax.ppermute(same, ("row", "col"), route(0))
    other = lax.ppermute(other, ("row", "col"), route(1))
    return jnp.stack(swap(same, other))


def panel_part(eta_pairs, gamma_pairs, pieces):
    whole = lax.all_gather(
        pieces.reshape(4 * COLS, PANEL_DEV), "row", axis=0, tiled=True
    ).reshape(N_COL, 2, COLS, PANEL_DEV)
    sums = pl.pallas_call(
        panel_kernel,
        grid=(N_COL // 2,),
        in_specs=[
            pl.BlockSpec((ROWS, COLS), lambda c: (0, 0)),
            pl.BlockSpec((ROWS, COLS), lambda c: (0, 0)),
            pl.BlockSpec((2, 2, COLS, PANEL_DEV), lambda c: (c, 0, 0, 0)),
        ],
        out_specs=pl.BlockSpec((2, ROWS, PANEL_DEV), lambda c: (c, 0, 0)),
        out_shape=jax.ShapeDtypeStruct((N_COL, ROWS, PANEL_DEV), bf16),
        compiler_params=params(),
        cost_estimate=pl.CostEstimate(
            flops=4 * ROWS * COLS * N_COL * PANEL_DEV, bytes_accessed=20 << 20, transcendentals=0
        ),
        name="panel",
    )(eta_pairs, gamma_pairs, whole)
    done = lax.psum_scatter(
        sums.reshape(N_COL * ROWS, PANEL_DEV), "col", scatter_dimension=0, tiled=True
    )
    return pl.pallas_call(
        turn_kernel,
        in_specs=[vmem_spec()],
        out_specs=vmem_spec(),
        out_shape=jax.ShapeDtypeStruct((PANEL_DEV, ROWS), bf16),
        compiler_params=params(),
        name="turn",
    )(done)


def exchange(tiles):
    return lax.all_to_all(tiles, ("row", "col"), split_axis=0, concat_axis=0, tiled=True)


def updates(
    eta_pairs,
    gamma_pairs,
    pieces,
    gamma_recoupled,
    ph_factor,
    tile_source,
    tile_owner,
    tile_place,
    sixj_weight,
    live_count,
):
    weights = sixj_weight.astype(f32)
    slots = BLOCKS * CAP
    groups = BLOCKS // GROUP
    rows = CAP * TILE
    dma = pltpu.SemaphoreType.DMA
    held = pltpu.VMEM((BLOCKS, rows, TILE), bf16)
    sent, tiles, factors = pl.pallas_call(
        send_kernel,
        in_specs=[smem_spec()] * 5 + [vmem_spec()],
        out_specs=[any_spec(), smem_spec(), smem_spec()],
        out_shape=[
            jax.ShapeDtypeStruct((BLOCKS, rows + CODE_ROWS, TILE), bf16),
            jax.ShapeDtypeStruct((slots,), jnp.int32),
            jax.ShapeDtypeStruct((slots,), f32),
        ],
        scratch_shapes=[
            pltpu.SMEM((slots,), jnp.int32),
            pltpu.SMEM((BLOCKS,), jnp.int32),
            pltpu.VMEM((BLOCKS, rows + CODE_ROWS, TILE), bf16),
            dma((groups,)),
        ],
        compiler_params=params(),
        cost_estimate=pl.CostEstimate(flops=0, bytes_accessed=11 << 20, transcendentals=0),
        name="send",
    )(live_count, tile_source, tile_owner, tile_place, weights, eta_pairs)
    sent, pieces = lax.optimization_barrier((sent, pieces))
    panel_update = panel_part(eta_pairs, gamma_pairs, pieces)
    received = exchange(sent)
    places = received[:, rows, :CAP].astype(jnp.int32).reshape(slots)
    places = places // PH_TILES * 16 + places % PH_TILES
    whole = (PH_STATES, PH_STATES)
    answers = pl.pallas_call(
        channel_kernel,
        in_specs=[smem_spec(), any_spec(), any_spec(), vmem_spec()],
        out_specs=any_spec(),
        out_shape=jax.ShapeDtypeStruct((BLOCKS, rows, TILE), bf16),
        scratch_shapes=[
            held,
            pltpu.VMEM(whole, bf16),
            pltpu.VMEM(whole, f32),
            pltpu.VMEM(whole, bf16),
            pltpu.VMEM(whole, bf16),
            dma((groups,)),
            dma,
            dma((groups,)),
        ],
        compiler_params=params(),
        cost_estimate=pl.CostEstimate(
            flops=4 * PH_STATES**3, bytes_accessed=22 << 20, transcendentals=0
        ),
        name="channel",
    )(places, received, gamma_recoupled[0], ph_factor.reshape(PH_STATES, 1))
    returned = exchange(answers)
    recoupled_update = pl.pallas_call(
        update_kernel,
        in_specs=[smem_spec(), smem_spec(), any_spec()],
        out_specs=vmem_spec(),
        out_shape=jax.ShapeDtypeStruct((ROWS, COLS), bf16),
        scratch_shapes=[held, pltpu.VMEM((ROWS, COLS), f32), dma((groups,))],
        compiler_params=params(),
        cost_estimate=pl.CostEstimate(flops=0, bytes_accessed=11 << 20, transcendentals=0),
        name="update",
    )(tiles, factors, returned)
    return (panel_update, recoupled_update)


def local(
    eta_pairs,
    gamma_pairs,
    pair_first,
    pair_second,
    occupancy,
    gamma_recoupled,
    ph_factor,
    tile_source,
    tile_owner,
    tile_place,
    sixj_weight,
    live_count,
):
    pieces = panel_pieces(eta_pairs, gamma_pairs, pair_first, pair_second, occupancy)
    return updates(
        eta_pairs,
        gamma_pairs,
        pieces,
        gamma_recoupled,
        ph_factor,
        tile_source,
        tile_owner,
        tile_place,
        sixj_weight,
        live_count,
    )


def solution(mesh):
    in_specs = (
        P("row", "col"),
        P("row", "col"),
        P("row"),
        P("row"),
        P(),
        P(("row", "col"), None, None),
        P(("row", "col"), None),
        P(("row", "col"), None),
        P(("row", "col"), None),
        P(("row", "col"), None),
        P(("row", "col"), None),
        P(("row", "col")),
    )
    out_specs = (P("col", "row"), P("row", "col"))
    return jax.shard_map(local, mesh=mesh, in_specs=in_specs, out_specs=out_specs, check_vma=False)
```

```python
import jax
import jax.numpy as jnp
from jax import lax
from jax.experimental import pallas as pl
from jax.experimental.pallas import tpu as pltpu
from jax.sharding import PartitionSpec as P

TILE = 128
ORBITS = 240
PH_STATES = 1536
PH_TILES = 12
PANEL_DEV = 128
ROWS = 1536
COLS = 768
COL_TILES = 6
TILES_BLOCK = 72
SLOTS = 144
BLOCKS = 128
CAP = 2
N_ROW = 8
N_COL = 16
SIDE = 4
GROUP = 16
CODE_ROWS = 8
VMEM_LIMIT = 60 * 1024 * 1024

f32 = jnp.float32
bf16 = jnp.bfloat16
SMEM = pltpu.MemorySpace.SMEM
VMEM = pltpu.MemorySpace.VMEM


def smem_spec():
    return pl.BlockSpec(memory_space=SMEM)


def any_spec():
    return pl.BlockSpec(memory_space=pl.ANY)


def vmem_spec():
    return pl.BlockSpec(memory_space=VMEM)


def params():
    return pltpu.CompilerParams(vmem_limit_bytes=VMEM_LIMIT)


def aligned(start, size):
    return pl.ds(pl.multiple_of(start * size, size), size)


def step_through(count, unroll, body):
    def step(i, carry):
        for j in range(unroll):
            body(i * unroll + j)
        return carry

    lax.fori_loop(0, count // unroll, step, 0)


def send_kernel(
    live_ref,
    source_ref,
    owner_ref,
    place_ref,
    weight_ref,
    eta_ref,
    out_ref,
    tile_ref,
    factor_ref,
    place_of,
    counts,
    held,
    sems,
):
    def clear(n):
        tile_ref[n] = 0
        factor_ref[n] = 0.0
        place_of[n] = 0

    step_through(BLOCKS * CAP, 8, clear)

    def clear_count(q):
        counts[q] = 0

    step_through(BLOCKS, 8, clear_count)

    def slot(s, carry):
        q = owner_ref[0, s]
        k = counts[q]
        counts[q] = k + 1
        n = q * CAP + k
        t = source_ref[0, s]
        r = t // COL_TILES
        tile_ref[n] = r * 8 + (t - r * COL_TILES)
        factor_ref[n] = weight_ref[0, s]
        u = place_ref[0, s]
        v = u // PH_TILES
        place_of[n] = v * 16 + (u - v * PH_TILES)
        return carry

    lax.fori_loop(0, live_ref[0], slot, 0)
    lane = lax.broadcasted_iota(jnp.int32, (CODE_ROWS, TILE), 1)

    def copy(j):
        part = pl.ds(j * GROUP, GROUP)
        return pltpu.make_async_copy(held.at[part], out_ref.at[part], sems.at[j])

    def group(j, carry):
        def owner(i):
            q = j * GROUP + i
            for k in range(CAP):
                n = q * CAP + k
                t = tile_ref[n]
                tile = eta_ref[aligned(t >> 3, TILE), aligned(t & 7, TILE)]
                held[q, k * TILE : (k + 1) * TILE, :] = (
                    factor_ref[n] * tile.astype(f32)
                ).astype(bf16)
            codes = jnp.where(lane == 0, place_of[q * CAP], place_of[q * CAP + 1])
            held[q, CAP * TILE : CAP * TILE + CODE_ROWS, :] = codes.astype(f32).astype(bf16)

        step_through(GROUP, 4, owner)
        copy(j).start()
        return carry

    lax.fori_loop(0, BLOCKS // GROUP, group, 0)

    def finish(j):
        copy(j).wait()

    step_through(BLOCKS // GROUP, 1, finish)


def update_kernel(tile_ref, factor_ref, back_ref, out_ref, held, total, sems):
    def copy(j):
        part = pl.ds(j * GROUP, GROUP)
        return pltpu.make_async_copy(back_ref.at[part], held.at[part], sems.at[j])

    def begin(j):
        copy(j).start()

    step_through(BLOCKS // GROUP, 1, begin)

    def clear(r):
        total[aligned(r, TILE), :] = jnp.zeros((TILE, COLS), f32)

    step_through(ROWS // TILE, 1, clear)

    def group(j, carry):
        copy(j).wait()

        def owner(i):
            q = j * GROUP + i
            for k in range(CAP):
                n = q * CAP + k
                t = tile_ref[n]
                rows, cols = aligned(t >> 3, TILE), aligned(t & 7, TILE)
                total[rows, cols] += factor_ref[n] * held[
                    q, k * TILE : (k + 1) * TILE, :
                ].astype(f32)

        step_through(GROUP, 4, owner)
        return carry

    lax.fori_loop(0, BLOCKS // GROUP, group, 0)

    def finish(r):
        rows = aligned(r, TILE)
        out_ref[rows, :] = total[rows, :].astype(bf16)

    step_through(ROWS // TILE, 1, finish)


def channel_kernel(
    place_ref,
    got_ref,
    gamma_hbm,
    scale_ref,
    out_ref,
    held,
    gamma_ref,
    total,
    eta,
    product,
    got_sems,
    gamma_sem,
    out_sems,
):
    def copy(j):
        part = pl.ds(j * GROUP, GROUP)
        return pltpu.make_async_copy(
            got_ref.at[part, pl.ds(0, CAP * TILE)], held.at[part], got_sems.at[j]
        )

    gamma_copy = pltpu.make_async_copy(gamma_hbm, gamma_ref, gamma_sem)

    def begin(j):
        copy(j).start()

    step_through(BLOCKS // GROUP, 1, begin)
    gamma_copy.start()

    def clear(r):
        total[aligned(r, TILE), :] = jnp.zeros((TILE, PH_STATES), f32)

    step_through(PH_TILES, 1, clear)

    def place(n):
        code = place_ref[n]
        return aligned(code >> 4, TILE), aligned(code & 15, TILE)

    def group(j, carry):
        copy(j).wait()

        def block(i):
            b = j * GROUP + i
            for k in range(CAP):
                rows, cols = place(b * CAP + k)
                total[rows, cols] += held[b, k * TILE : (k + 1) * TILE, :].astype(f32)

        step_through(GROUP, 4, block)
        return carry

    lax.fori_loop(0, BLOCKS // GROUP, group, 0)

    def settle(r):
        rows = aligned(r, TILE)
        eta[rows, :] = total[rows, :].astype(bf16)

    step_through(PH_TILES, 1, settle)
    gamma_copy.wait()
    width = 256

    def multiply(c):
        cols = aligned(c, width)
        scale = scale_ref[...]
        gamma_scaled = (scale * gamma_ref[:, cols].astype(f32)).astype(bf16)
        eta_scaled = (-scale * eta[:, cols].astype(f32)).astype(bf16)
        part = jnp.dot(eta[...], gamma_scaled, preferred_element_type=f32)
        part += jnp.dot(gamma_ref[...], eta_scaled, preferred_element_type=f32)
        product[:, cols] = part.astype(bf16)

    step_through(PH_STATES // width, 1, multiply)

    def back(j):
        part = pl.ds(j * GROUP, GROUP)
        return pltpu.make_async_copy(held.at[part], out_ref.at[part], out_sems.at[j])

    def answers(j, carry):
        def block(i):
            b = j * GROUP + i
            for k in range(CAP):
                rows, cols = place(b * CAP + k)
                held[b, k * TILE : (k + 1) * TILE, :] = product[rows, cols]

        step_through(GROUP, 4, block)
        back(j).start()
        return carry

    lax.fori_loop(0, BLOCKS // GROUP, answers, 0)

    def finish(j):
        back(j).wait()

    step_through(BLOCKS // GROUP, 1, finish)


def panel_kernel(x_ref, eta_ref, gamma_ref, panel_ref, out_ref):
    gamma_cols = jnp.concatenate([panel_ref[0, 0], panel_ref[1, 0]], axis=1)
    eta_cols = jnp.concatenate([panel_ref[0, 1], panel_ref[1, 1]], axis=1)
    part = jnp.dot(eta_ref[...], gamma_cols, preferred_element_type=f32)
    part -= jnp.dot(gamma_ref[...], eta_cols, preferred_element_type=f32)
    part = part.astype(bf16)
    for k in range(2):
        out_ref[k] = part[:, k * PANEL_DEV : (k + 1) * PANEL_DEV]


def turn_kernel(in_ref, out_ref):
    out_ref[...] = in_ref[...].astype(f32).T.astype(bf16)


def orbit_lookup(pair_ids, occupancy):
    orbit_ids = jnp.arange(occupancy.shape[0], dtype=jnp.int32)
    return jnp.sum(
        jnp.where(pair_ids[:, None] == orbit_ids[None, :], occupancy[None, :], 0.0), axis=1
    )


def panel_pieces(eta_pairs, gamma_pairs, pair_first, pair_second, occupancy):
    factor = 1.0 - orbit_lookup(pair_first, occupancy) - orbit_lookup(pair_second, occupancy)

    def weigh(pairs):
        return (factor[:, None] * pairs[:, :PANEL_DEV].astype(f32)).astype(bf16)

    halves = jnp.stack([weigh(gamma_pairs), weigh(eta_pairs)]).reshape(2, 2, COLS, PANEL_DEV)
    odd = lax.axis_index("col") % 2 == 1

    def swap(first, second):
        return jnp.where(odd, second, first), jnp.where(odd, first, second)

    def turned(i, c):
        return 2 * ((i // 2 + c // SIDE) % SIDE) + c % SIDE // 2

    def route(flip):
        return [
            (i * N_COL + c, turned(i, c) * N_COL + 2 * i + (c + flip) % 2)
            for i in range(N_ROW)
            for c in range(N_COL)
        ]

    same, other = swap(halves[:, 0], halves[:, 1])
    same = lax.ppermute(same, ("row", "col"), route(0))
    other = lax.ppermute(other, ("row", "col"), route(1))
    return jnp.stack(swap(same, other))


def panel_part(eta_pairs, gamma_pairs, pieces):
    whole = lax.all_gather(
        pieces.reshape(4 * COLS, PANEL_DEV), "row", axis=0, tiled=True
    ).reshape(N_COL, 2, COLS, PANEL_DEV)
    sums = pl.pallas_call(
        panel_kernel,
        grid_spec=pltpu.PrefetchScalarGridSpec(
            num_scalar_prefetch=1,
            grid=(SIDE, 2),
            in_specs=[
                pl.BlockSpec((ROWS, COLS), lambda y, h, x: (0, 0)),
                pl.BlockSpec((ROWS, COLS), lambda y, h, x: (0, 0)),
                pl.BlockSpec(
                    (2, 2, COLS, PANEL_DEV),
                    lambda y, h, x: (2 * lax.rem(y + x[0], SIDE) + h, 0, 0, 0),
                ),
            ],
            out_specs=pl.BlockSpec((2, ROWS, PANEL_DEV), lambda y, h, x: (2 * y + h, 0, 0)),
        ),
        out_shape=jax.ShapeDtypeStruct((N_COL, ROWS, PANEL_DEV), bf16),
        compiler_params=params(),
        cost_estimate=pl.CostEstimate(
            flops=4 * ROWS * COLS * N_COL * PANEL_DEV, bytes_accessed=20 << 20, transcendentals=0
        ),
        name="panel",
    )((lax.axis_index("col") // SIDE).reshape(1), eta_pairs, gamma_pairs, whole)
    done = lax.psum_scatter(
        sums.reshape(N_COL * ROWS, PANEL_DEV), "col", scatter_dimension=0, tiled=True
    )
    return pl.pallas_call(
        turn_kernel,
        in_specs=[vmem_spec()],
        out_specs=vmem_spec(),
        out_shape=jax.ShapeDtypeStruct((PANEL_DEV, ROWS), bf16),
        compiler_params=params(),
        name="turn",
    )(done)


def exchange(tiles):
    return lax.all_to_all(tiles, ("row", "col"), split_axis=0, concat_axis=0, tiled=True)


def updates(
    eta_pairs,
    gamma_pairs,
    pieces,
    gamma_recoupled,
    ph_factor,
    tile_source,
    tile_owner,
    tile_place,
    sixj_weight,
    live_count,
):
    weights = sixj_weight.astype(f32)
    slots = BLOCKS * CAP
    groups = BLOCKS // GROUP
    rows = CAP * TILE
    dma = pltpu.SemaphoreType.DMA
    held = pltpu.VMEM((BLOCKS, rows, TILE), bf16)
    sent, tiles, factors = pl.pallas_call(
        send_kernel,
        in_specs=[smem_spec()] * 5 + [vmem_spec()],
        out_specs=[any_spec(), smem_spec(), smem_spec()],
        out_shape=[
            jax.ShapeDtypeStruct((BLOCKS, rows + CODE_ROWS, TILE), bf16),
            jax.ShapeDtypeStruct((slots,), jnp.int32),
            jax.ShapeDtypeStruct((slots,), f32),
        ],
        scratch_shapes=[
            pltpu.SMEM((slots,), jnp.int32),
            pltpu.SMEM((BLOCKS,), jnp.int32),
            pltpu.VMEM((BLOCKS, rows + CODE_ROWS, TILE), bf16),
            dma((groups,)),
        ],
        compiler_params=params(),
        cost_estimate=pl.CostEstimate(flops=0, bytes_accessed=11 << 20, transcendentals=0),
        name="send",
    )(live_count, tile_source, tile_owner, tile_place, weights, eta_pairs)
    sent, pieces = lax.optimization_barrier((sent, pieces))
    panel_update = panel_part(eta_pairs, gamma_pairs, pieces)
    received = exchange(sent)
    places = received[:, rows, :CAP].astype(jnp.int32).reshape(slots)
    whole = (PH_STATES, PH_STATES)
    answers = pl.pallas_call(
        channel_kernel,
        in_specs=[smem_spec(), any_spec(), any_spec(), vmem_spec()],
        out_specs=any_spec(),
        out_shape=jax.ShapeDtypeStruct((BLOCKS, rows, TILE), bf16),
        scratch_shapes=[
            held,
            pltpu.VMEM(whole, bf16),
            pltpu.VMEM(whole, f32),
            pltpu.VMEM(whole, bf16),
            pltpu.VMEM(whole, bf16),
            dma((groups,)),
            dma,
            dma((groups,)),
        ],
        compiler_params=params(),
        cost_estimate=pl.CostEstimate(
            flops=4 * PH_STATES**3, bytes_accessed=22 << 20, transcendentals=0
        ),
        name="channel",
    )(places, received, gamma_recoupled[0], ph_factor.reshape(PH_STATES, 1))
    returned = exchange(answers)
    recoupled_update = pl.pallas_call(
        update_kernel,
        in_specs=[smem_spec(), smem_spec(), any_spec()],
        out_specs=vmem_spec(),
        out_shape=jax.ShapeDtypeStruct((ROWS, COLS), bf16),
        scratch_shapes=[held, pltpu.VMEM((ROWS, COLS), f32), dma((groups,))],
        compiler_params=params(),
        cost_estimate=pl.CostEstimate(flops=0, bytes_accessed=11 << 20, transcendentals=0),
        name="update",
    )(tiles, factors, returned)
    return (panel_update, recoupled_update)


def local(
    eta_pairs,
    gamma_pairs,
    pair_first,
    pair_second,
    occupancy,
    gamma_recoupled,
    ph_factor,
    tile_source,
    tile_owner,
    tile_place,
    sixj_weight,
    live_count,
):
    pieces = panel_pieces(eta_pairs, gamma_pairs, pair_first, pair_second, occupancy)
    return updates(
        eta_pairs,
        gamma_pairs,
        pieces,
        gamma_recoupled,
        ph_factor,
        tile_source,
        tile_owner,
        tile_place,
        sixj_weight,
        live_count,
    )


def solution(mesh):
    in_specs = (
        P("row", "col"),
        P("row", "col"),
        P("row"),
        P("row"),
        P(),
        P(("row", "col"), None, None),
        P(("row", "col"), None),
        P(("row", "col"), None),
        P(("row", "col"), None),
        P(("row", "col"), None),
        P(("row", "col"), None),
        P(("row", "col")),
    )
    out_specs = (P("col", "row"), P("row", "col"))
    return jax.shard_map(local, mesh=mesh, in_specs=in_specs, out_specs=out_specs, check_vma=False)
```

```python
import jax
import jax.numpy as jnp
from jax import lax
from jax.experimental import pallas as pl
from jax.experimental.pallas import tpu as pltpu
from jax.sharding import PartitionSpec as P

TILE = 128
ORBITS = 240
PH_STATES = 1536
PH_TILES = 12
PANEL_DEV = 128
ROWS = 1536
COLS = 768
COL_TILES = 6
TILES_BLOCK = 72
SLOTS = 144
BLOCKS = 128
CAP = 2
N_ROW = 8
N_COL = 16
SIDE = 4
GROUP = 16
CODE_ROWS = 8
VMEM_LIMIT = 60 * 1024 * 1024

f32 = jnp.float32
bf16 = jnp.bfloat16
SMEM = pltpu.MemorySpace.SMEM
VMEM = pltpu.MemorySpace.VMEM


def smem_spec():
    return pl.BlockSpec(memory_space=SMEM)


def any_spec():
    return pl.BlockSpec(memory_space=pl.ANY)


def vmem_spec():
    return pl.BlockSpec(memory_space=VMEM)


def params():
    return pltpu.CompilerParams(vmem_limit_bytes=VMEM_LIMIT)


def aligned(start, size):
    return pl.ds(pl.multiple_of(start * size, size), size)


def step_through(count, unroll, body):
    def step(i, carry):
        for j in range(unroll):
            body(i * unroll + j)
        return carry

    lax.fori_loop(0, count // unroll, step, 0)


def send_kernel(
    live_ref,
    source_ref,
    owner_ref,
    place_ref,
    weight_ref,
    eta_hbm,
    out_ref,
    tile_ref,
    factor_ref,
    place_of,
    counts,
    held,
    eta_ref,
    sems,
    eta_sem,
):
    eta_copy = pltpu.make_async_copy(eta_hbm, eta_ref, eta_sem)
    eta_copy.start()

    def clear(n):
        tile_ref[n] = 0
        factor_ref[n] = 0.0
        place_of[n] = 0

    step_through(BLOCKS * CAP, 8, clear)

    def clear_count(q):
        counts[q] = 0

    step_through(BLOCKS, 8, clear_count)

    def slot(s, carry):
        q = owner_ref[0, s]
        k = counts[q]
        counts[q] = k + 1
        n = q * CAP + k
        t = source_ref[0, s]
        r = t // COL_TILES
        tile_ref[n] = r * 8 + (t - r * COL_TILES)
        factor_ref[n] = weight_ref[0, s]
        u = place_ref[0, s]
        v = u // PH_TILES
        place_of[n] = v * 16 + (u - v * PH_TILES)
        return carry

    lax.fori_loop(0, live_ref[0], slot, 0)
    lane = lax.broadcasted_iota(jnp.int32, (CODE_ROWS, TILE), 1)
    eta_copy.wait()

    def copy(j):
        part = pl.ds(j * GROUP, GROUP)
        return pltpu.make_async_copy(held.at[part], out_ref.at[part], sems.at[j])

    def group(j, carry):
        def owner(i):
            q = j * GROUP + i
            for k in range(CAP):
                n = q * CAP + k
                t = tile_ref[n]
                tile = eta_ref[aligned(t >> 3, TILE), aligned(t & 7, TILE)]
                held[q, k * TILE : (k + 1) * TILE, :] = (
                    factor_ref[n] * tile.astype(f32)
                ).astype(bf16)
            codes = jnp.where(lane == 0, place_of[q * CAP], place_of[q * CAP + 1])
            held[q, CAP * TILE : CAP * TILE + CODE_ROWS, :] = codes.astype(f32).astype(bf16)

        step_through(GROUP, 4, owner)
        copy(j).start()
        return carry

    lax.fori_loop(0, BLOCKS // GROUP, group, 0)

    def finish(j):
        copy(j).wait()

    step_through(BLOCKS // GROUP, 1, finish)


def update_kernel(
    tile_ref, factor_ref, back_ref, sums_ref, out_ref, turned_ref, held, total, other, sems
):
    def copy(j):
        part = pl.ds(j * GROUP, GROUP)
        return pltpu.make_async_copy(back_ref.at[part], held.at[part], sems.at[j])

    def begin(j):
        copy(j).start()

    step_through(BLOCKS // GROUP, 1, begin)

    def clear(r):
        total[aligned(r, TILE), :] = jnp.zeros((TILE, COLS), f32)
        other[aligned(r, TILE), :] = jnp.zeros((TILE, COLS), f32)

    step_through(ROWS // TILE, 1, clear)
    turned_ref[...] = sums_ref[...].astype(f32).T.astype(bf16)

    def group(j, carry):
        copy(j).wait()

        def owner(i):
            q = j * GROUP + i
            for k, into in enumerate((total, other)):
                n = q * CAP + k
                t = tile_ref[n]
                rows, cols = aligned(t >> 3, TILE), aligned(t & 7, TILE)
                into[rows, cols] += factor_ref[n] * held[
                    q, k * TILE : (k + 1) * TILE, :
                ].astype(f32)

        step_through(GROUP, 4, owner)
        return carry

    lax.fori_loop(0, BLOCKS // GROUP, group, 0)

    def finish(r):
        rows = aligned(r, TILE)
        out_ref[rows, :] = (total[rows, :] + other[rows, :]).astype(bf16)

    step_through(ROWS // TILE, 1, finish)


def channel_kernel(
    place_ref,
    got_ref,
    gamma_hbm,
    scale_ref,
    out_ref,
    held,
    gamma_ref,
    total,
    eta,
    product,
    got_sems,
    gamma_sem,
    out_sems,
):
    def copy(j):
        part = pl.ds(j * GROUP, GROUP)
        return pltpu.make_async_copy(
            got_ref.at[part, pl.ds(0, CAP * TILE)], held.at[part], got_sems.at[j]
        )

    gamma_copy = pltpu.make_async_copy(gamma_hbm, gamma_ref, gamma_sem)

    def begin(j):
        copy(j).start()

    step_through(BLOCKS // GROUP, 1, begin)
    gamma_copy.start()

    def clear(r):
        total[aligned(r, TILE), :] = jnp.zeros((TILE, PH_STATES), f32)

    step_through(PH_TILES, 1, clear)

    def place(n):
        code = place_ref[n]
        return aligned(code >> 4, TILE), aligned(code & 15, TILE)

    def group(j, carry):
        copy(j).wait()

        def block(i):
            b = j * GROUP + i
            for k in range(CAP):
                rows, cols = place(b * CAP + k)
                total[rows, cols] += held[b, k * TILE : (k + 1) * TILE, :].astype(f32)

        step_through(GROUP, 4, block)
        return carry

    lax.fori_loop(0, BLOCKS // GROUP, group, 0)

    def settle(r):
        rows = aligned(r, TILE)
        eta[rows, :] = total[rows, :].astype(bf16)

    step_through(PH_TILES, 1, settle)
    gamma_copy.wait()
    width = 256

    def multiply(c):
        cols = aligned(c, width)
        scale = scale_ref[...]
        gamma_scaled = (scale * gamma_ref[:, cols].astype(f32)).astype(bf16)
        eta_scaled = (-scale * eta[:, cols].astype(f32)).astype(bf16)
        part = jnp.dot(eta[...], gamma_scaled, preferred_element_type=f32)
        part += jnp.dot(gamma_ref[...], eta_scaled, preferred_element_type=f32)
        product[:, cols] = part.astype(bf16)

    step_through(PH_STATES // width, 1, multiply)

    def back(j):
        part = pl.ds(j * GROUP, GROUP)
        return pltpu.make_async_copy(held.at[part], out_ref.at[part], out_sems.at[j])

    def answers(j, carry):
        def block(i):
            b = j * GROUP + i
            for k in range(CAP):
                rows, cols = place(b * CAP + k)
                held[b, k * TILE : (k + 1) * TILE, :] = product[rows, cols]

        step_through(GROUP, 4, block)
        back(j).start()
        return carry

    lax.fori_loop(0, BLOCKS // GROUP, answers, 0)

    def finish(j):
        back(j).wait()

    step_through(BLOCKS // GROUP, 1, finish)


def panel_kernel(x_ref, eta_ref, gamma_ref, panel_ref, out_ref):
    gamma_cols = jnp.concatenate([panel_ref[k, 0] for k in range(SIDE)], axis=1)
    eta_cols = jnp.concatenate([panel_ref[k, 1] for k in range(SIDE)], axis=1)
    part = jnp.dot(eta_ref[...], gamma_cols, preferred_element_type=f32)
    part -= jnp.dot(gamma_ref[...], eta_cols, preferred_element_type=f32)
    part = part.astype(bf16)
    for k in range(SIDE):
        out_ref[k] = part[:, k * PANEL_DEV : (k + 1) * PANEL_DEV]


def orbit_lookup(pair_ids, occupancy):
    orbit_ids = jnp.arange(occupancy.shape[0], dtype=jnp.int32)
    return jnp.sum(
        jnp.where(pair_ids[:, None] == orbit_ids[None, :], occupancy[None, :], 0.0), axis=1
    )


def panel_pieces(eta_pairs, gamma_pairs, pair_first, pair_second, occupancy):
    factor = 1.0 - orbit_lookup(pair_first, occupancy) - orbit_lookup(pair_second, occupancy)

    def weigh(pairs):
        return (factor[:, None] * pairs[:, :PANEL_DEV].astype(f32)).astype(bf16)

    halves = jnp.stack([weigh(gamma_pairs), weigh(eta_pairs)]).reshape(2, 2, COLS, PANEL_DEV)
    odd = lax.axis_index("col") % 2 == 1

    def swap(first, second):
        return jnp.where(odd, second, first), jnp.where(odd, first, second)

    def target(i, c, h):
        x = (i // 2 + c // SIDE + i % 2 + 2 * h) % SIDE
        return (2 * x + c % SIDE // 2) * N_COL + 2 * i + h

    def route(flip):
        return [
            (i * N_COL + c, target(i, c, (c + flip) % 2))
            for i in range(N_ROW)
            for c in range(N_COL)
        ]

    same, other = swap(halves[:, 0], halves[:, 1])
    same = lax.ppermute(same, ("row", "col"), route(0))
    other = lax.ppermute(other, ("row", "col"), route(1))
    return jnp.stack(swap(same, other))


def panel_part(eta_pairs, gamma_pairs, pieces):
    whole = lax.all_gather(
        pieces.reshape(4 * COLS, PANEL_DEV), "row", axis=0, tiled=True
    ).reshape(N_COL, 2, COLS, PANEL_DEV)
    me = lax.axis_index("col")
    turn = me // SIDE + me // 2 % 2 + me % 2 * 2
    sums = pl.pallas_call(
        panel_kernel,
        grid_spec=pltpu.PrefetchScalarGridSpec(
            num_scalar_prefetch=1,
            grid=(SIDE,),
            in_specs=[
                pl.BlockSpec((ROWS, COLS), lambda y, x: (0, 0)),
                pl.BlockSpec((ROWS, COLS), lambda y, x: (0, 0)),
                pl.BlockSpec(
                    (SIDE, 2, COLS, PANEL_DEV),
                    lambda y, x: (lax.rem(y + x[0], SIDE), 0, 0, 0),
                ),
            ],
            out_specs=pl.BlockSpec((SIDE, ROWS, PANEL_DEV), lambda y, x: (y, 0, 0)),
        ),
        out_shape=jax.ShapeDtypeStruct((N_COL, ROWS, PANEL_DEV), bf16),
        compiler_params=params(),
        cost_estimate=pl.CostEstimate(
            flops=4 * ROWS * COLS * N_COL * PANEL_DEV, bytes_accessed=20 << 20, transcendentals=0
        ),
        name="panel",
    )(turn.reshape(1), eta_pairs, gamma_pairs, whole)
    return lax.psum_scatter(
        sums.reshape(N_COL * ROWS, PANEL_DEV), "col", scatter_dimension=0, tiled=True
    )


def exchange(tiles):
    return lax.all_to_all(tiles, ("row", "col"), split_axis=0, concat_axis=0, tiled=True)


def updates(
    eta_pairs,
    gamma_pairs,
    pieces,
    gamma_recoupled,
    ph_factor,
    tile_source,
    tile_owner,
    tile_place,
    sixj_weight,
    live_count,
):
    weights = sixj_weight.astype(f32)
    slots = BLOCKS * CAP
    groups = BLOCKS // GROUP
    rows = CAP * TILE
    dma = pltpu.SemaphoreType.DMA
    held = pltpu.VMEM((BLOCKS, rows, TILE), bf16)
    sent, tiles, factors = pl.pallas_call(
        send_kernel,
        in_specs=[smem_spec()] * 5 + [any_spec()],
        out_specs=[any_spec(), smem_spec(), smem_spec()],
        out_shape=[
            jax.ShapeDtypeStruct((BLOCKS, rows + CODE_ROWS, TILE), bf16),
            jax.ShapeDtypeStruct((slots,), jnp.int32),
            jax.ShapeDtypeStruct((slots,), f32),
        ],
        scratch_shapes=[
            pltpu.SMEM((slots,), jnp.int32),
            pltpu.SMEM((BLOCKS,), jnp.int32),
            pltpu.VMEM((BLOCKS, rows + CODE_ROWS, TILE), bf16),
            pltpu.VMEM((ROWS, COLS), bf16),
            dma((groups,)),
            dma,
        ],
        compiler_params=params(),
        cost_estimate=pl.CostEstimate(flops=0, bytes_accessed=11 << 20, transcendentals=0),
        name="send",
    )(live_count, tile_source, tile_owner, tile_place, weights, eta_pairs)
    sent, pieces = lax.optimization_barrier((sent, pieces))
    panel_sums = panel_part(eta_pairs, gamma_pairs, pieces)
    received = exchange(sent)
    places = received[:, rows, :CAP].astype(jnp.int32).reshape(slots)
    whole = (PH_STATES, PH_STATES)
    answers = pl.pallas_call(
        channel_kernel,
        in_specs=[smem_spec(), any_spec(), any_spec(), vmem_spec()],
        out_specs=any_spec(),
        out_shape=jax.ShapeDtypeStruct((BLOCKS, rows, TILE), bf16),
        scratch_shapes=[
            held,
            pltpu.VMEM(whole, bf16),
            pltpu.VMEM(whole, f32),
            pltpu.VMEM(whole, bf16),
            pltpu.VMEM(whole, bf16),
            dma((groups,)),
            dma,
            dma((groups,)),
        ],
        compiler_params=params(),
        cost_estimate=pl.CostEstimate(
            flops=4 * PH_STATES**3, bytes_accessed=22 << 20, transcendentals=0
        ),
        name="channel",
    )(places, received, gamma_recoupled[0], ph_factor.reshape(PH_STATES, 1))
    returned = exchange(answers)
    recoupled_update, panel_update = pl.pallas_call(
        update_kernel,
        in_specs=[smem_spec(), smem_spec(), any_spec(), vmem_spec()],
        out_specs=[vmem_spec(), vmem_spec()],
        out_shape=[
            jax.ShapeDtypeStruct((ROWS, COLS), bf16),
            jax.ShapeDtypeStruct((PANEL_DEV, ROWS), bf16),
        ],
        scratch_shapes=[held] + [pltpu.VMEM((ROWS, COLS), f32)] * 2 + [dma((groups,))],
        compiler_params=params(),
        cost_estimate=pl.CostEstimate(flops=0, bytes_accessed=11 << 20, transcendentals=0),
        name="update",
    )(tiles, factors, returned, panel_sums)
    return (panel_update, recoupled_update)


def local(
    eta_pairs,
    gamma_pairs,
    pair_first,
    pair_second,
    occupancy,
    gamma_recoupled,
    ph_factor,
    tile_source,
    tile_owner,
    tile_place,
    sixj_weight,
    live_count,
):
    pieces = panel_pieces(eta_pairs, gamma_pairs, pair_first, pair_second, occupancy)
    return updates(
        eta_pairs,
        gamma_pairs,
        pieces,
        gamma_recoupled,
        ph_factor,
        tile_source,
        tile_owner,
        tile_place,
        sixj_weight,
        live_count,
    )


def solution(mesh):
    in_specs = (
        P("row", "col"),
        P("row", "col"),
        P("row"),
        P("row"),
        P(),
        P(("row", "col"), None, None),
        P(("row", "col"), None),
        P(("row", "col"), None),
        P(("row", "col"), None),
        P(("row", "col"), None),
        P(("row", "col"), None),
        P(("row", "col")),
    )
    out_specs = (P("col", "row"), P("row", "col"))
    return jax.shard_map(local, mesh=mesh, in_specs=in_specs, out_specs=out_specs, check_vma=False)
```

```python
import jax
import jax.numpy as jnp
from jax import lax
from jax.experimental import pallas as pl
from jax.experimental.pallas import tpu as pltpu
from jax.sharding import PartitionSpec as P

TILE = 128
ORBITS = 240
PH_STATES = 1536
PH_TILES = 12
PANEL_DEV = 128
ROWS = 1536
COLS = 768
COL_TILES = 6
TILES_BLOCK = 72
SLOTS = 144
BLOCKS = 128
CAP = 2
N_ROW = 8
N_COL = 16
SIDE = 4
GROUP = 16
CODE_ROWS = 8
VMEM_LIMIT = 60 * 1024 * 1024

f32 = jnp.float32
bf16 = jnp.bfloat16
SMEM = pltpu.MemorySpace.SMEM
VMEM = pltpu.MemorySpace.VMEM


def smem_spec():
    return pl.BlockSpec(memory_space=SMEM)


def any_spec():
    return pl.BlockSpec(memory_space=pl.ANY)


def vmem_spec():
    return pl.BlockSpec(memory_space=VMEM)


def params():
    return pltpu.CompilerParams(vmem_limit_bytes=VMEM_LIMIT)


def aligned(start, size):
    return pl.ds(pl.multiple_of(start * size, size), size)


def step_through(count, unroll, body):
    def step(i, carry):
        for j in range(unroll):
            body(i * unroll + j)
        return carry

    lax.fori_loop(0, count // unroll, step, 0)


def send_kernel(
    live_ref,
    source_ref,
    owner_ref,
    place_ref,
    weight_ref,
    eta_hbm,
    out_ref,
    tile_ref,
    factor_ref,
    place_of,
    counts,
    held,
    eta_ref,
    sems,
    eta_sem,
):
    eta_copy = pltpu.make_async_copy(eta_hbm, eta_ref, eta_sem)
    eta_copy.start()

    def clear(n):
        tile_ref[n] = 0
        factor_ref[n] = 0.0
        place_of[n] = 0

    step_through(BLOCKS * CAP, 8, clear)

    def clear_count(q):
        counts[q] = 0

    step_through(BLOCKS, 8, clear_count)

    def slot(s, carry):
        q = owner_ref[0, s]
        k = counts[q]
        counts[q] = k + 1
        n = q * CAP + k
        t = source_ref[0, s]
        r = t // COL_TILES
        tile_ref[n] = r * 8 + (t - r * COL_TILES)
        factor_ref[n] = weight_ref[0, s]
        u = place_ref[0, s]
        v = u // PH_TILES
        place_of[n] = v * 16 + (u - v * PH_TILES)
        return carry

    lax.fori_loop(0, live_ref[0], slot, 0)
    lane = lax.broadcasted_iota(jnp.int32, (CODE_ROWS, TILE), 1)
    eta_copy.wait()

    def copy(j):
        part = pl.ds(j * GROUP, GROUP)
        return pltpu.make_async_copy(held.at[part], out_ref.at[part], sems.at[j])

    def group(j, carry):
        def owner(i):
            q = j * GROUP + i
            for k in range(CAP):
                n = q * CAP + k
                t = tile_ref[n]
                tile = eta_ref[aligned(t >> 3, TILE), aligned(t & 7, TILE)]
                held[q, k * TILE : (k + 1) * TILE, :] = (
                    factor_ref[n] * tile.astype(f32)
                ).astype(bf16)
            codes = jnp.where(lane == 0, place_of[q * CAP], place_of[q * CAP + 1])
            held[q, CAP * TILE : CAP * TILE + CODE_ROWS, :] = codes.astype(f32).astype(bf16)

        step_through(GROUP, 4, owner)
        copy(j).start()
        return carry

    lax.fori_loop(0, BLOCKS // GROUP, group, 0)

    def finish(j):
        copy(j).wait()

    step_through(BLOCKS // GROUP, 1, finish)


def update_kernel(
    tile_ref, factor_ref, back_ref, sums_ref, out_ref, turned_ref, held, total, other, sems
):
    def copy(j):
        part = pl.ds(j * GROUP, GROUP)
        return pltpu.make_async_copy(back_ref.at[part], held.at[part], sems.at[j])

    def begin(j):
        copy(j).start()

    step_through(BLOCKS // GROUP, 1, begin)

    def clear(r):
        total[aligned(r, TILE), :] = jnp.zeros((TILE, COLS), f32)
        other[aligned(r, TILE), :] = jnp.zeros((TILE, COLS), f32)

    step_through(ROWS // TILE, 1, clear)
    turned_ref[...] = sums_ref[...].astype(f32).T.astype(bf16)

    def group(j, carry):
        copy(j).wait()

        def owner(i):
            q = j * GROUP + i
            for k, into in enumerate((total, other)):
                n = q * CAP + k
                t = tile_ref[n]
                rows, cols = aligned(t >> 3, TILE), aligned(t & 7, TILE)
                into[rows, cols] += factor_ref[n] * held[
                    q, k * TILE : (k + 1) * TILE, :
                ].astype(f32)

        step_through(GROUP, 4, owner)
        return carry

    lax.fori_loop(0, BLOCKS // GROUP, group, 0)

    def finish(r):
        rows = aligned(r, TILE)
        out_ref[rows, :] = (total[rows, :] + other[rows, :]).astype(bf16)

    step_through(ROWS // TILE, 1, finish)


def channel_kernel(
    got_ref,
    gamma_hbm,
    scale_ref,
    out_ref,
    held,
    gamma_ref,
    total,
    eta,
    product,
    code_rows,
    codes,
    place_ref,
    got_sems,
    gamma_sem,
    out_sems,
    code_sem,
):
    code_copy = pltpu.make_async_copy(
        got_ref.at[:, pl.ds(CAP * TILE, CODE_ROWS)], code_rows, code_sem
    )
    code_copy.start()

    def copy(j):
        part = pl.ds(j * GROUP, GROUP)
        return pltpu.make_async_copy(
            got_ref.at[part, pl.ds(0, CAP * TILE)], held.at[part], got_sems.at[j]
        )

    gamma_copy = pltpu.make_async_copy(gamma_hbm, gamma_ref, gamma_sem)

    def begin(j):
        copy(j).start()

    step_through(BLOCKS // GROUP, 1, begin)
    gamma_copy.start()
    code_copy.wait()
    codes[...] = code_rows[:, 0, :].astype(f32).astype(jnp.int32)
    place_copy = pltpu.make_async_copy(codes, place_ref, code_sem)
    place_copy.start()

    def clear(r):
        total[aligned(r, TILE), :] = jnp.zeros((TILE, PH_STATES), f32)

    step_through(PH_TILES, 1, clear)
    place_copy.wait()

    def place(b, k):
        code = place_ref[b, k]
        return aligned(code >> 4, TILE), aligned(code & 15, TILE)

    def group(j, carry):
        copy(j).wait()

        def block(i):
            b = j * GROUP + i
            for k in range(CAP):
                rows, cols = place(b, k)
                total[rows, cols] += held[b, k * TILE : (k + 1) * TILE, :].astype(f32)

        step_through(GROUP, 4, block)
        return carry

    lax.fori_loop(0, BLOCKS // GROUP, group, 0)

    def settle(r):
        rows = aligned(r, TILE)
        eta[rows, :] = total[rows, :].astype(bf16)

    step_through(PH_TILES, 1, settle)
    gamma_copy.wait()
    width = 768

    def multiply(c):
        cols = aligned(c, width)
        scale = scale_ref[...]
        gamma_scaled = (scale * gamma_ref[:, cols].astype(f32)).astype(bf16)
        eta_scaled = (-scale * eta[:, cols].astype(f32)).astype(bf16)
        part = jnp.dot(eta[...], gamma_scaled, preferred_element_type=f32)
        part += jnp.dot(gamma_ref[...], eta_scaled, preferred_element_type=f32)
        product[:, cols] = part.astype(bf16)

    step_through(PH_STATES // width, 1, multiply)

    def back(j):
        part = pl.ds(j * GROUP, GROUP)
        return pltpu.make_async_copy(held.at[part], out_ref.at[part], out_sems.at[j])

    def answers(j, carry):
        def block(i):
            b = j * GROUP + i
            for k in range(CAP):
                rows, cols = place(b, k)
                held[b, k * TILE : (k + 1) * TILE, :] = product[rows, cols]

        step_through(GROUP, 4, block)
        back(j).start()
        return carry

    lax.fori_loop(0, BLOCKS // GROUP, answers, 0)

    def finish(j):
        back(j).wait()

    step_through(BLOCKS // GROUP, 1, finish)


def panel_kernel(x_ref, eta_ref, gamma_ref, panel_ref, out_ref):
    gamma_cols = jnp.concatenate([panel_ref[k, 0] for k in range(SIDE)], axis=1)
    eta_cols = jnp.concatenate([panel_ref[k, 1] for k in range(SIDE)], axis=1)
    part = jnp.dot(eta_ref[...], gamma_cols, preferred_element_type=f32)
    part -= jnp.dot(gamma_ref[...], eta_cols, preferred_element_type=f32)
    part = part.astype(bf16)
    for k in range(SIDE):
        out_ref[k] = part[:, k * PANEL_DEV : (k + 1) * PANEL_DEV]


def orbit_lookup(pair_ids, occupancy):
    orbit_ids = jnp.arange(occupancy.shape[0], dtype=jnp.int32)
    return jnp.sum(
        jnp.where(pair_ids[:, None] == orbit_ids[None, :], occupancy[None, :], 0.0), axis=1
    )


def panel_pieces(eta_pairs, gamma_pairs, pair_first, pair_second, occupancy):
    factor = 1.0 - orbit_lookup(pair_first, occupancy) - orbit_lookup(pair_second, occupancy)

    def weigh(pairs):
        return (factor[:, None] * pairs[:, :PANEL_DEV].astype(f32)).astype(bf16)

    halves = jnp.stack([weigh(gamma_pairs), weigh(eta_pairs)]).reshape(2, 2, COLS, PANEL_DEV)
    odd = lax.axis_index("col") % 2 == 1

    def swap(first, second):
        return jnp.where(odd, second, first), jnp.where(odd, first, second)

    def target(i, c, h):
        x = (i // 2 + c // SIDE + i % 2 + 2 * h) % SIDE
        return (2 * x + c % SIDE // 2) * N_COL + 2 * i + h

    def route(flip):
        return [
            (i * N_COL + c, target(i, c, (c + flip) % 2))
            for i in range(N_ROW)
            for c in range(N_COL)
        ]

    same, other = swap(halves[:, 0], halves[:, 1])
    same = lax.ppermute(same, ("row", "col"), route(0))
    other = lax.ppermute(other, ("row", "col"), route(1))
    return jnp.stack(swap(same, other))


def panel_part(eta_pairs, gamma_pairs, pieces):
    whole = lax.all_gather(
        pieces.reshape(4 * COLS, PANEL_DEV), "row", axis=0, tiled=True
    ).reshape(N_COL, 2, COLS, PANEL_DEV)
    me = lax.axis_index("col")
    turn = me // SIDE + me // 2 % 2 + me % 2 * 2
    sums = pl.pallas_call(
        panel_kernel,
        grid_spec=pltpu.PrefetchScalarGridSpec(
            num_scalar_prefetch=1,
            grid=(SIDE,),
            in_specs=[
                pl.BlockSpec((ROWS, COLS), lambda y, x: (0, 0)),
                pl.BlockSpec((ROWS, COLS), lambda y, x: (0, 0)),
                pl.BlockSpec(
                    (SIDE, 2, COLS, PANEL_DEV),
                    lambda y, x: (lax.rem(y + x[0], SIDE), 0, 0, 0),
                ),
            ],
            out_specs=pl.BlockSpec((SIDE, ROWS, PANEL_DEV), lambda y, x: (y, 0, 0)),
        ),
        out_shape=jax.ShapeDtypeStruct((N_COL, ROWS, PANEL_DEV), bf16),
        compiler_params=params(),
        cost_estimate=pl.CostEstimate(
            flops=4 * ROWS * COLS * N_COL * PANEL_DEV, bytes_accessed=20 << 20, transcendentals=0
        ),
        name="panel",
    )(turn.reshape(1), eta_pairs, gamma_pairs, whole)
    return lax.psum_scatter(
        sums.reshape(N_COL * ROWS, PANEL_DEV), "col", scatter_dimension=0, tiled=True
    )


def exchange(tiles):
    return lax.all_to_all(tiles, ("row", "col"), split_axis=0, concat_axis=0, tiled=True)


def updates(
    eta_pairs,
    gamma_pairs,
    pieces,
    gamma_recoupled,
    ph_factor,
    tile_source,
    tile_owner,
    tile_place,
    sixj_weight,
    live_count,
):
    weights = sixj_weight.astype(f32)
    slots = BLOCKS * CAP
    groups = BLOCKS // GROUP
    rows = CAP * TILE
    dma = pltpu.SemaphoreType.DMA
    held = pltpu.VMEM((BLOCKS, rows, TILE), bf16)
    sent, tiles, factors = pl.pallas_call(
        send_kernel,
        in_specs=[smem_spec()] * 5 + [any_spec()],
        out_specs=[any_spec(), smem_spec(), smem_spec()],
        out_shape=[
            jax.ShapeDtypeStruct((BLOCKS, rows + CODE_ROWS, TILE), bf16),
            jax.ShapeDtypeStruct((slots,), jnp.int32),
            jax.ShapeDtypeStruct((slots,), f32),
        ],
        scratch_shapes=[
            pltpu.SMEM((slots,), jnp.int32),
            pltpu.SMEM((BLOCKS,), jnp.int32),
            pltpu.VMEM((BLOCKS, rows + CODE_ROWS, TILE), bf16),
            pltpu.VMEM((ROWS, COLS), bf16),
            dma((groups,)),
            dma,
        ],
        compiler_params=params(),
        cost_estimate=pl.CostEstimate(flops=0, bytes_accessed=11 << 20, transcendentals=0),
        name="send",
    )(live_count, tile_source, tile_owner, tile_place, weights, eta_pairs)
    sent, pieces = lax.optimization_barrier((sent, pieces))
    panel_sums = panel_part(eta_pairs, gamma_pairs, pieces)
    received = exchange(sent)
    whole = (PH_STATES, PH_STATES)
    answers = pl.pallas_call(
        channel_kernel,
        in_specs=[any_spec(), any_spec(), vmem_spec()],
        out_specs=any_spec(),
        out_shape=jax.ShapeDtypeStruct((BLOCKS, rows, TILE), bf16),
        scratch_shapes=[
            held,
            pltpu.VMEM(whole, bf16),
            pltpu.VMEM(whole, f32),
            pltpu.VMEM(whole, bf16),
            pltpu.VMEM(whole, bf16),
            pltpu.VMEM((BLOCKS, CODE_ROWS, TILE), bf16),
            pltpu.VMEM((BLOCKS, TILE), jnp.int32),
            pltpu.SMEM((BLOCKS, TILE), jnp.int32),
            dma((groups,)),
            dma,
            dma((groups,)),
            dma,
        ],
        compiler_params=params(),
        cost_estimate=pl.CostEstimate(
            flops=4 * PH_STATES**3, bytes_accessed=22 << 20, transcendentals=0
        ),
        name="channel",
    )(received, gamma_recoupled[0], ph_factor.reshape(PH_STATES, 1))
    returned = exchange(answers)
    recoupled_update, panel_update = pl.pallas_call(
        update_kernel,
        in_specs=[smem_spec(), smem_spec(), any_spec(), vmem_spec()],
        out_specs=[vmem_spec(), vmem_spec()],
        out_shape=[
            jax.ShapeDtypeStruct((ROWS, COLS), bf16),
            jax.ShapeDtypeStruct((PANEL_DEV, ROWS), bf16),
        ],
        scratch_shapes=[held] + [pltpu.VMEM((ROWS, COLS), f32)] * 2 + [dma((groups,))],
        compiler_params=params(),
        cost_estimate=pl.CostEstimate(flops=0, bytes_accessed=11 << 20, transcendentals=0),
        name="update",
    )(tiles, factors, returned, panel_sums)
    return (panel_update, recoupled_update)


def local(
    eta_pairs,
    gamma_pairs,
    pair_first,
    pair_second,
    occupancy,
    gamma_recoupled,
    ph_factor,
    tile_source,
    tile_owner,
    tile_place,
    sixj_weight,
    live_count,
):
    pieces = panel_pieces(eta_pairs, gamma_pairs, pair_first, pair_second, occupancy)
    return updates(
        eta_pairs,
        gamma_pairs,
        pieces,
        gamma_recoupled,
        ph_factor,
        tile_source,
        tile_owner,
        tile_place,
        sixj_weight,
        live_count,
    )


def solution(mesh):
    in_specs = (
        P("row", "col"),
        P("row", "col"),
        P("row"),
        P("row"),
        P(),
        P(("row", "col"), None, None),
        P(("row", "col"), None),
        P(("row", "col"), None),
        P(("row", "col"), None),
        P(("row", "col"), None),
        P(("row", "col"), None),
        P(("row", "col")),
    )
    out_specs = (P("col", "row"), P("row", "col"))
    return jax.shard_map(local, mesh=mesh, in_specs=in_specs, out_specs=out_specs, check_vma=False)
```

```python
import jax
import jax.numpy as jnp
from jax import lax
from jax.experimental import pallas as pl
from jax.experimental.pallas import tpu as pltpu
from jax.sharding import PartitionSpec as P

TILE = 128
ORBITS = 240
PH_STATES = 1536
PH_TILES = 12
PANEL_DEV = 128
ROWS = 1536
COLS = 768
COL_TILES = 6
TILES_BLOCK = 72
SLOTS = 144
BLOCKS = 128
CAP = 2
N_ROW = 8
N_COL = 16
SIDE = 4
GROUP = 16
CODE_ROWS = 8
VMEM_LIMIT = 60 * 1024 * 1024

f32 = jnp.float32
bf16 = jnp.bfloat16
SMEM = pltpu.MemorySpace.SMEM
VMEM = pltpu.MemorySpace.VMEM


def smem_spec():
    return pl.BlockSpec(memory_space=SMEM)


def any_spec():
    return pl.BlockSpec(memory_space=pl.ANY)


def vmem_spec():
    return pl.BlockSpec(memory_space=VMEM)


def params():
    return pltpu.CompilerParams(vmem_limit_bytes=VMEM_LIMIT)


def aligned(start, size):
    return pl.ds(pl.multiple_of(start * size, size), size)


def step_through(count, unroll, body):
    def step(i, carry):
        for j in range(unroll):
            body(i * unroll + j)
        return carry

    lax.fori_loop(0, count // unroll, step, 0)


def send_kernel(
    live_ref,
    source_ref,
    owner_ref,
    place_ref,
    weight_ref,
    eta_hbm,
    out_ref,
    tile_ref,
    factor_ref,
    place_of,
    counts,
    held,
    eta_ref,
    sems,
    eta_sem,
):
    eta_copy = pltpu.make_async_copy(eta_hbm, eta_ref, eta_sem)
    eta_copy.start()

    def clear(n):
        tile_ref[n] = 0
        factor_ref[n] = 0.0
        place_of[n] = 0

    step_through(BLOCKS * CAP, 8, clear)

    def clear_count(q):
        counts[q] = 0

    step_through(BLOCKS, 8, clear_count)

    def slot(s, carry):
        q = owner_ref[0, s]
        k = counts[q]
        counts[q] = k + 1
        n = q * CAP + k
        t = source_ref[0, s]
        r = t // COL_TILES
        tile_ref[n] = r * 8 + (t - r * COL_TILES)
        factor_ref[n] = weight_ref[0, s]
        u = place_ref[0, s]
        v = u // PH_TILES
        place_of[n] = v * 16 + (u - v * PH_TILES)
        return carry

    lax.fori_loop(0, live_ref[0], slot, 0)
    lane = lax.broadcasted_iota(jnp.int32, (CODE_ROWS, TILE), 1)
    eta_copy.wait()

    def copy(j):
        part = pl.ds(j * GROUP, GROUP)
        return pltpu.make_async_copy(held.at[part], out_ref.at[part], sems.at[j])

    def group(j, carry):
        def owner(i):
            q = j * GROUP + i
            for k in range(CAP):
                n = q * CAP + k
                t = tile_ref[n]
                tile = eta_ref[aligned(t >> 3, TILE), aligned(t & 7, TILE)]
                held[q, k * TILE : (k + 1) * TILE, :] = (
                    factor_ref[n] * tile.astype(f32)
                ).astype(bf16)
            codes = jnp.where(lane == 0, place_of[q * CAP], place_of[q * CAP + 1])
            held[q, CAP * TILE : CAP * TILE + CODE_ROWS, :] = codes.astype(f32).astype(bf16)

        step_through(GROUP, 4, owner)
        copy(j).start()
        return carry

    lax.fori_loop(0, BLOCKS // GROUP, group, 0)

    def finish(j):
        copy(j).wait()

    step_through(BLOCKS // GROUP, 1, finish)


def update_kernel(
    tile_ref, factor_ref, back_ref, sums_ref, out_ref, turned_ref, held, total, used, sems
):
    def copy(j):
        part = pl.ds(j * GROUP, GROUP)
        return pltpu.make_async_copy(back_ref.at[part], held.at[part], sems.at[j])

    def begin(j):
        copy(j).start()

    step_through(BLOCKS // GROUP, 1, begin)

    def note(i, count):
        for j in range(8):
            n = i * 8 + j
            used[count] = n
            count = count + (factor_ref[n] != 0.0).astype(jnp.int32)
        return count

    count = lax.fori_loop(0, BLOCKS * CAP // 8, note, 0)

    def clear(r):
        total[aligned(r, TILE), :] = jnp.zeros((TILE, COLS), f32)

    step_through(ROWS // TILE, 1, clear)
    turned_ref[...] = sums_ref[...].astype(f32).T.astype(bf16)

    def arrive(j, carry):
        copy(j).wait()
        return carry

    batch = 8

    def add(i, arrived):
        last = used[jnp.minimum(i * batch + batch, count) - 1]
        needed = last // (GROUP * CAP) + 1
        lax.fori_loop(arrived, needed, arrive, 0)
        for j in range(batch):
            e = i * batch + j
            n = jnp.where(e < count, used[e], 0)
            factor = jnp.where(e < count, factor_ref[n], 0.0)
            t = tile_ref[n]
            rows, cols = aligned(t >> 3, TILE), aligned(t & 7, TILE)
            at = pl.ds(pl.multiple_of((n & 1) * TILE, TILE), TILE)
            total[rows, cols] += factor * held[n >> 1, at, :].astype(f32)
        return jnp.maximum(arrived, needed)

    arrived = lax.fori_loop(0, (count + batch - 1) // batch, add, 0)
    lax.fori_loop(arrived, BLOCKS // GROUP, arrive, 0)

    def finish(r):
        rows = aligned(r, TILE)
        out_ref[rows, :] = total[rows, :].astype(bf16)

    step_through(ROWS // TILE, 1, finish)


def channel_kernel(
    got_ref,
    gamma_hbm,
    scale_ref,
    out_ref,
    held,
    gamma_ref,
    total,
    eta,
    product,
    code_rows,
    codes,
    place_ref,
    got_sems,
    gamma_sem,
    out_sems,
    code_sem,
):
    code_copy = pltpu.make_async_copy(
        got_ref.at[:, pl.ds(CAP * TILE, CODE_ROWS)], code_rows, code_sem
    )
    code_copy.start()

    def copy(j):
        part = pl.ds(j * GROUP, GROUP)
        return pltpu.make_async_copy(
            got_ref.at[part, pl.ds(0, CAP * TILE)], held.at[part], got_sems.at[j]
        )

    gamma_copy = pltpu.make_async_copy(gamma_hbm, gamma_ref, gamma_sem)

    def begin(j):
        copy(j).start()

    step_through(BLOCKS // GROUP, 1, begin)
    gamma_copy.start()
    code_copy.wait()
    codes[...] = code_rows[:, 0, :].astype(f32).astype(jnp.int32)
    place_copy = pltpu.make_async_copy(codes, place_ref, code_sem)
    place_copy.start()

    def clear(r):
        total[aligned(r, TILE), :] = jnp.zeros((TILE, PH_STATES), f32)

    step_through(PH_TILES, 1, clear)
    place_copy.wait()

    def place(b, k):
        code = place_ref[b, k]
        return aligned(code >> 4, TILE), aligned(code & 15, TILE)

    def group(j, carry):
        copy(j).wait()

        def block(i):
            b = j * GROUP + i
            for k in range(CAP):
                rows, cols = place(b, k)
                total[rows, cols] += held[b, k * TILE : (k + 1) * TILE, :].astype(f32)

        step_through(GROUP, 4, block)
        return carry

    lax.fori_loop(0, BLOCKS // GROUP, group, 0)

    def settle(r):
        rows = aligned(r, TILE)
        eta[rows, :] = total[rows, :].astype(bf16)

    step_through(PH_TILES, 1, settle)
    gamma_copy.wait()
    width = 768

    def multiply(c):
        cols = aligned(c, width)
        scale = scale_ref[...]
        gamma_scaled = (scale * gamma_ref[:, cols].astype(f32)).astype(bf16)
        eta_scaled = (-scale * eta[:, cols].astype(f32)).astype(bf16)
        for h in range(2):
            rows = pl.ds(h * width, width)
            part = jnp.dot(eta[rows, :], gamma_scaled, preferred_element_type=f32)
            part += jnp.dot(gamma_ref[rows, :], eta_scaled, preferred_element_type=f32)
            product[rows, cols] = part.astype(bf16)

    step_through(PH_STATES // width, 1, multiply)

    def back(j):
        part = pl.ds(j * GROUP, GROUP)
        return pltpu.make_async_copy(held.at[part], out_ref.at[part], out_sems.at[j])

    def answers(j, carry):
        def block(i):
            b = j * GROUP + i
            for k in range(CAP):
                rows, cols = place(b, k)
                held[b, k * TILE : (k + 1) * TILE, :] = product[rows, cols]

        step_through(GROUP, 4, block)
        back(j).start()
        return carry

    lax.fori_loop(0, BLOCKS // GROUP, answers, 0)

    def finish(j):
        back(j).wait()

    step_through(BLOCKS // GROUP, 1, finish)


def panel_kernel(x_ref, eta_ref, gamma_ref, panel_ref, out_ref):
    gamma_cols = jnp.concatenate([panel_ref[k, 0] for k in range(SIDE)], axis=1)
    eta_cols = jnp.concatenate([panel_ref[k, 1] for k in range(SIDE)], axis=1)
    part = jnp.dot(eta_ref[...], gamma_cols, preferred_element_type=f32)
    part -= jnp.dot(gamma_ref[...], eta_cols, preferred_element_type=f32)
    part = part.astype(bf16)
    for k in range(SIDE):
        out_ref[k] = part[:, k * PANEL_DEV : (k + 1) * PANEL_DEV]


def orbit_lookup(pair_ids, occupancy):
    orbit_ids = jnp.arange(occupancy.shape[0], dtype=jnp.int32)
    return jnp.sum(
        jnp.where(pair_ids[:, None] == orbit_ids[None, :], occupancy[None, :], 0.0), axis=1
    )


def panel_pieces(eta_pairs, gamma_pairs, pair_first, pair_second, occupancy):
    factor = 1.0 - orbit_lookup(pair_first, occupancy) - orbit_lookup(pair_second, occupancy)

    def weigh(pairs):
        return (factor[:, None] * pairs[:, :PANEL_DEV].astype(f32)).astype(bf16)

    halves = jnp.stack([weigh(gamma_pairs), weigh(eta_pairs)]).reshape(2, 2, COLS, PANEL_DEV)
    odd = lax.axis_index("col") % 2 == 1

    def swap(first, second):
        return jnp.where(odd, second, first), jnp.where(odd, first, second)

    def target(i, c, h):
        x = (i // 2 + c // SIDE + i % 2 + 2 * h) % SIDE
        return (2 * x + c % SIDE // 2) * N_COL + 2 * i + h

    def route(flip):
        return [
            (i * N_COL + c, target(i, c, (c + flip) % 2))
            for i in range(N_ROW)
            for c in range(N_COL)
        ]

    same, other = swap(halves[:, 0], halves[:, 1])
    same = lax.ppermute(same, ("row", "col"), route(0))
    other = lax.ppermute(other, ("row", "col"), route(1))
    return jnp.stack(swap(same, other))


def panel_part(eta_pairs, gamma_pairs, pieces):
    whole = lax.all_gather(
        pieces.reshape(4 * COLS, PANEL_DEV), "row", axis=0, tiled=True
    ).reshape(N_COL, 2, COLS, PANEL_DEV)
    me = lax.axis_index("col")
    turn = me // SIDE + me // 2 % 2 + me % 2 * 2
    sums = pl.pallas_call(
        panel_kernel,
        grid_spec=pltpu.PrefetchScalarGridSpec(
            num_scalar_prefetch=1,
            grid=(SIDE,),
            in_specs=[
                pl.BlockSpec((ROWS, COLS), lambda y, x: (0, 0)),
                pl.BlockSpec((ROWS, COLS), lambda y, x: (0, 0)),
                pl.BlockSpec(
                    (SIDE, 2, COLS, PANEL_DEV),
                    lambda y, x: (lax.rem(y + x[0], SIDE), 0, 0, 0),
                ),
            ],
            out_specs=pl.BlockSpec((SIDE, ROWS, PANEL_DEV), lambda y, x: (y, 0, 0)),
        ),
        out_shape=jax.ShapeDtypeStruct((N_COL, ROWS, PANEL_DEV), bf16),
        compiler_params=params(),
        cost_estimate=pl.CostEstimate(
            flops=4 * ROWS * COLS * N_COL * PANEL_DEV, bytes_accessed=20 << 20, transcendentals=0
        ),
        name="panel",
    )(turn.reshape(1), eta_pairs, gamma_pairs, whole)
    return lax.psum_scatter(
        sums.reshape(N_COL * ROWS, PANEL_DEV), "col", scatter_dimension=0, tiled=True
    )


def exchange(tiles):
    return lax.all_to_all(tiles, ("row", "col"), split_axis=0, concat_axis=0, tiled=True)


def updates(
    eta_pairs,
    gamma_pairs,
    pieces,
    gamma_recoupled,
    ph_factor,
    tile_source,
    tile_owner,
    tile_place,
    sixj_weight,
    live_count,
):
    weights = sixj_weight.astype(f32)
    slots = BLOCKS * CAP
    groups = BLOCKS // GROUP
    rows = CAP * TILE
    dma = pltpu.SemaphoreType.DMA
    held = pltpu.VMEM((BLOCKS, rows, TILE), bf16)
    sent, tiles, factors = pl.pallas_call(
        send_kernel,
        in_specs=[smem_spec()] * 5 + [any_spec()],
        out_specs=[any_spec(), smem_spec(), smem_spec()],
        out_shape=[
            jax.ShapeDtypeStruct((BLOCKS, rows + CODE_ROWS, TILE), bf16),
            jax.ShapeDtypeStruct((slots,), jnp.int32),
            jax.ShapeDtypeStruct((slots,), f32),
        ],
        scratch_shapes=[
            pltpu.SMEM((slots,), jnp.int32),
            pltpu.SMEM((BLOCKS,), jnp.int32),
            pltpu.VMEM((BLOCKS, rows + CODE_ROWS, TILE), bf16),
            pltpu.VMEM((ROWS, COLS), bf16),
            dma((groups,)),
            dma,
        ],
        compiler_params=params(),
        cost_estimate=pl.CostEstimate(flops=0, bytes_accessed=11 << 20, transcendentals=0),
        name="send",
    )(live_count, tile_source, tile_owner, tile_place, weights, eta_pairs)
    sent, pieces = lax.optimization_barrier((sent, pieces))
    panel_sums = panel_part(eta_pairs, gamma_pairs, pieces)
    received = exchange(sent)
    whole = (PH_STATES, PH_STATES)
    answers = pl.pallas_call(
        channel_kernel,
        in_specs=[any_spec(), any_spec(), vmem_spec()],
        out_specs=any_spec(),
        out_shape=jax.ShapeDtypeStruct((BLOCKS, rows, TILE), bf16),
        scratch_shapes=[
            held,
            pltpu.VMEM(whole, bf16),
            pltpu.VMEM(whole, f32),
            pltpu.VMEM(whole, bf16),
            pltpu.VMEM(whole, bf16),
            pltpu.VMEM((BLOCKS, CODE_ROWS, TILE), bf16),
            pltpu.VMEM((BLOCKS, TILE), jnp.int32),
            pltpu.SMEM((BLOCKS, TILE), jnp.int32),
            dma((groups,)),
            dma,
            dma((groups,)),
            dma,
        ],
        compiler_params=params(),
        cost_estimate=pl.CostEstimate(
            flops=4 * PH_STATES**3, bytes_accessed=22 << 20, transcendentals=0
        ),
        name="channel",
    )(received, gamma_recoupled[0], ph_factor.reshape(PH_STATES, 1))
    returned = exchange(answers)
    recoupled_update, panel_update = pl.pallas_call(
        update_kernel,
        in_specs=[smem_spec(), smem_spec(), any_spec(), vmem_spec()],
        out_specs=[vmem_spec(), vmem_spec()],
        out_shape=[
            jax.ShapeDtypeStruct((ROWS, COLS), bf16),
            jax.ShapeDtypeStruct((PANEL_DEV, ROWS), bf16),
        ],
        scratch_shapes=[
            held,
            pltpu.VMEM((ROWS, COLS), f32),
            pltpu.SMEM((slots + 8,), jnp.int32),
            dma((groups,)),
        ],
        compiler_params=params(),
        cost_estimate=pl.CostEstimate(flops=0, bytes_accessed=11 << 20, transcendentals=0),
        name="update",
    )(tiles, factors, returned, panel_sums)
    return (panel_update, recoupled_update)


def local(
    eta_pairs,
    gamma_pairs,
    pair_first,
    pair_second,
    occupancy,
    gamma_recoupled,
    ph_factor,
    tile_source,
    tile_owner,
    tile_place,
    sixj_weight,
    live_count,
):
    pieces = panel_pieces(eta_pairs, gamma_pairs, pair_first, pair_second, occupancy)
    return updates(
        eta_pairs,
        gamma_pairs,
        pieces,
        gamma_recoupled,
        ph_factor,
        tile_source,
        tile_owner,
        tile_place,
        sixj_weight,
        live_count,
    )


def solution(mesh):
    in_specs = (
        P("row", "col"),
        P("row", "col"),
        P("row"),
        P("row"),
        P(),
        P(("row", "col"), None, None),
        P(("row", "col"), None),
        P(("row", "col"), None),
        P(("row", "col"), None),
        P(("row", "col"), None),
        P(("row", "col"), None),
        P(("row", "col")),
    )
    out_specs = (P("col", "row"), P("row", "col"))
    return jax.shard_map(local, mesh=mesh, in_specs=in_specs, out_specs=out_specs, check_vma=False)
```

```python
import jax
import jax.numpy as jnp
from jax import lax
from jax.experimental import pallas as pl
from jax.experimental.pallas import tpu as pltpu
from jax.sharding import PartitionSpec as P

TILE = 128
ORBITS = 240
PH_STATES = 1536
PH_TILES = 12
PANEL_DEV = 128
ROWS = 1536
COLS = 768
COL_TILES = 6
TILES_BLOCK = 72
SLOTS = 144
BLOCKS = 128
CAP = 2
N_ROW = 8
N_COL = 16
SIDE = 4
GROUP = 16
CODE_ROWS = 8
VMEM_LIMIT = 60 * 1024 * 1024

f32 = jnp.float32
bf16 = jnp.bfloat16
SMEM = pltpu.MemorySpace.SMEM
VMEM = pltpu.MemorySpace.VMEM


def smem_spec():
    return pl.BlockSpec(memory_space=SMEM)


def any_spec():
    return pl.BlockSpec(memory_space=pl.ANY)


def vmem_spec():
    return pl.BlockSpec(memory_space=VMEM)


def params():
    return pltpu.CompilerParams(vmem_limit_bytes=VMEM_LIMIT)


def aligned(start, size):
    return pl.ds(pl.multiple_of(start * size, size), size)


def step_through(count, unroll, body):
    def step(i, carry):
        for j in range(unroll):
            body(i * unroll + j)
        return carry

    lax.fori_loop(0, count // unroll, step, 0)


def send_kernel(
    live_ref,
    source_ref,
    owner_ref,
    place_ref,
    weight_ref,
    eta_hbm,
    out_ref,
    tile_ref,
    factor_ref,
    place_of,
    counts,
    held,
    eta_ref,
    sems,
    eta_sem,
):
    eta_copy = pltpu.make_async_copy(eta_hbm, eta_ref, eta_sem)
    eta_copy.start()

    def clear(n):
        tile_ref[n] = 0
        factor_ref[n] = 0.0
        place_of[n] = 0

    step_through(BLOCKS * CAP, 8, clear)

    def clear_count(q):
        counts[q] = 0

    step_through(BLOCKS, 8, clear_count)

    def slot(s, carry):
        owner = owner_ref[0, s]
        q = (owner & (N_COL - 1)) * N_ROW + owner // N_COL
        k = counts[q]
        counts[q] = k + 1
        n = q * CAP + k
        t = source_ref[0, s]
        r = t // COL_TILES
        tile_ref[n] = r * 8 + (t - r * COL_TILES)
        factor_ref[n] = weight_ref[0, s]
        u = place_ref[0, s]
        v = u // PH_TILES
        place_of[n] = v * 16 + (u - v * PH_TILES)
        return carry

    lax.fori_loop(0, live_ref[0], slot, 0)
    lane = lax.broadcasted_iota(jnp.int32, (CODE_ROWS, TILE), 1)
    eta_copy.wait()

    def copy(j):
        part = pl.ds(j * GROUP, GROUP)
        return pltpu.make_async_copy(held.at[part], out_ref.at[part], sems.at[j])

    def group(j, carry):
        def owner(i):
            q = j * GROUP + i
            for k in range(CAP):
                n = q * CAP + k
                t = tile_ref[n]
                tile = eta_ref[aligned(t >> 3, TILE), aligned(t & 7, TILE)]
                held[q, k * TILE : (k + 1) * TILE, :] = (
                    factor_ref[n] * tile.astype(f32)
                ).astype(bf16)
            codes = jnp.where(lane == 0, place_of[q * CAP], place_of[q * CAP + 1])
            held[q, CAP * TILE : CAP * TILE + CODE_ROWS, :] = codes.astype(f32).astype(bf16)

        step_through(GROUP, 4, owner)
        copy(j).start()
        return carry

    lax.fori_loop(0, BLOCKS // GROUP, group, 0)

    def finish(j):
        copy(j).wait()

    step_through(BLOCKS // GROUP, 1, finish)


def turn_kernel(in_ref, out_ref):
    out_ref[...] = in_ref[...].astype(f32).T.astype(bf16)


def update_kernel(
    tile_ref, factor_ref, back_ref, out_ref, held, total, used, sems
):
    def copy(j):
        part = pl.ds(j * GROUP, GROUP)
        return pltpu.make_async_copy(back_ref.at[part], held.at[part], sems.at[j])

    def begin(j):
        copy(j).start()

    step_through(BLOCKS // GROUP, 1, begin)

    def note(i, count):
        for j in range(8):
            n = i * 8 + j
            used[count] = n
            count = count + (factor_ref[n] != 0.0).astype(jnp.int32)
        return count

    count = lax.fori_loop(0, BLOCKS * CAP // 8, note, 0)

    def clear(r):
        total[aligned(r, TILE), :] = jnp.zeros((TILE, COLS), f32)

    step_through(ROWS // TILE, 1, clear)

    def arrive(j, carry):
        copy(j).wait()
        return carry

    batch = 8

    def add(i, arrived):
        last = used[jnp.minimum(i * batch + batch, count) - 1]
        needed = last // (GROUP * CAP) + 1
        lax.fori_loop(arrived, needed, arrive, 0)
        for j in range(batch):
            e = i * batch + j
            n = jnp.where(e < count, used[e], 0)
            factor = jnp.where(e < count, factor_ref[n], 0.0)
            t = tile_ref[n]
            rows, cols = aligned(t >> 3, TILE), aligned(t & 7, TILE)
            at = pl.ds(pl.multiple_of((n & 1) * TILE, TILE), TILE)
            total[rows, cols] += factor * held[n >> 1, at, :].astype(f32)
        return jnp.maximum(arrived, needed)

    arrived = lax.fori_loop(0, (count + batch - 1) // batch, add, 0)
    lax.fori_loop(arrived, BLOCKS // GROUP, arrive, 0)

    def finish(r):
        rows = aligned(r, TILE)
        out_ref[rows, :] = total[rows, :].astype(bf16)

    step_through(ROWS // TILE, 1, finish)


def channel_kernel(
    got_ref,
    gamma_hbm,
    scale_ref,
    out_ref,
    held,
    gamma_ref,
    total,
    eta,
    product,
    code_rows,
    codes,
    place_ref,
    got_sems,
    gamma_sem,
    out_sems,
    code_sem,
):
    code_copy = pltpu.make_async_copy(
        got_ref.at[:, pl.ds(CAP * TILE, CODE_ROWS)], code_rows, code_sem
    )
    code_copy.start()

    def copy(j):
        part = pl.ds(j * GROUP, GROUP)
        return pltpu.make_async_copy(
            got_ref.at[part, pl.ds(0, CAP * TILE)], held.at[part], got_sems.at[j]
        )

    gamma_copy = pltpu.make_async_copy(gamma_hbm, gamma_ref, gamma_sem)

    def begin(j):
        copy(j).start()

    step_through(BLOCKS // GROUP, 1, begin)
    gamma_copy.start()
    code_copy.wait()
    codes[...] = code_rows[:, 0, :].astype(f32).astype(jnp.int32)
    place_copy = pltpu.make_async_copy(codes, place_ref, code_sem)
    place_copy.start()

    def clear(r):
        total[aligned(r, TILE), :] = jnp.zeros((TILE, PH_STATES), f32)

    step_through(PH_TILES, 1, clear)
    place_copy.wait()

    def place(b, k):
        code = place_ref[b, k]
        return aligned(code >> 4, TILE), aligned(code & 15, TILE)

    def group(j, carry):
        copy(j).wait()

        def block(i):
            b = j * GROUP + i
            for k in range(CAP):
                rows, cols = place(b, k)
                total[rows, cols] += held[b, k * TILE : (k + 1) * TILE, :].astype(f32)

        step_through(GROUP, 4, block)
        return carry

    lax.fori_loop(0, BLOCKS // GROUP, group, 0)

    def settle(r):
        rows = aligned(r, TILE)
        eta[rows, :] = total[rows, :].astype(bf16)

    step_through(PH_TILES, 1, settle)
    gamma_copy.wait()
    width = 768

    def multiply(c):
        cols = aligned(c, width)
        scale = scale_ref[...]
        gamma_scaled = (scale * gamma_ref[:, cols].astype(f32)).astype(bf16)
        eta_scaled = (-scale * eta[:, cols].astype(f32)).astype(bf16)
        for h in range(2):
            rows = pl.ds(h * width, width)
            part = jnp.dot(eta[rows, :], gamma_scaled, preferred_element_type=f32)
            part += jnp.dot(gamma_ref[rows, :], eta_scaled, preferred_element_type=f32)
            product[rows, cols] = part.astype(bf16)

    step_through(PH_STATES // width, 1, multiply)

    def back(j):
        part = pl.ds(j * GROUP, GROUP)
        return pltpu.make_async_copy(held.at[part], out_ref.at[part], out_sems.at[j])

    def answers(j, carry):
        def block(i):
            b = j * GROUP + i
            for k in range(CAP):
                rows, cols = place(b, k)
                held[b, k * TILE : (k + 1) * TILE, :] = product[rows, cols]

        step_through(GROUP, 4, block)
        back(j).start()
        return carry

    lax.fori_loop(0, BLOCKS // GROUP, answers, 0)

    def finish(j):
        back(j).wait()

    step_through(BLOCKS // GROUP, 1, finish)


def panel_kernel(x_ref, eta_ref, gamma_ref, panel_ref, out_ref):
    gamma_cols = jnp.concatenate([panel_ref[k, 0] for k in range(SIDE)], axis=1)
    eta_cols = jnp.concatenate([panel_ref[k, 1] for k in range(SIDE)], axis=1)
    part = jnp.dot(eta_ref[...], gamma_cols, preferred_element_type=f32)
    part -= jnp.dot(gamma_ref[...], eta_cols, preferred_element_type=f32)
    part = part.astype(bf16)
    for k in range(SIDE):
        out_ref[k] = part[:, k * PANEL_DEV : (k + 1) * PANEL_DEV]


def orbit_lookup(pair_ids, occupancy):
    orbit_ids = jnp.arange(occupancy.shape[0], dtype=jnp.int32)
    return jnp.sum(
        jnp.where(pair_ids[:, None] == orbit_ids[None, :], occupancy[None, :], 0.0), axis=1
    )


def panel_pieces(eta_pairs, gamma_pairs, pair_first, pair_second, occupancy):
    factor = 1.0 - orbit_lookup(pair_first, occupancy) - orbit_lookup(pair_second, occupancy)

    def weigh(pairs):
        return (factor[:, None] * pairs[:, :PANEL_DEV].astype(f32)).astype(bf16)

    halves = jnp.stack([weigh(gamma_pairs), weigh(eta_pairs)]).reshape(2, 2, COLS, PANEL_DEV)
    odd = lax.axis_index("col") % 2 == 1

    def swap(first, second):
        return jnp.where(odd, second, first), jnp.where(odd, first, second)

    def target(i, c, h):
        x = (i // 2 + c // SIDE + i % 2 + 2 * h) % SIDE
        return (2 * x + c % SIDE // 2) * N_COL + 2 * i + h

    def route(flip):
        return [
            (i * N_COL + c, target(i, c, (c + flip) % 2))
            for i in range(N_ROW)
            for c in range(N_COL)
        ]

    same, other = swap(halves[:, 0], halves[:, 1])
    same = lax.ppermute(same, ("row", "col"), route(0))
    other = lax.ppermute(other, ("row", "col"), route(1))
    return jnp.stack(swap(same, other))


def panel_part(eta_pairs, gamma_pairs, pieces):
    whole = lax.all_gather(
        pieces.reshape(4 * COLS, PANEL_DEV), "row", axis=0, tiled=True
    ).reshape(N_COL, 2, COLS, PANEL_DEV)
    me = lax.axis_index("col")
    turn = me // SIDE + me // 2 % 2 + me % 2 * 2
    sums = pl.pallas_call(
        panel_kernel,
        grid_spec=pltpu.PrefetchScalarGridSpec(
            num_scalar_prefetch=1,
            grid=(SIDE,),
            in_specs=[
                pl.BlockSpec((ROWS, COLS), lambda y, x: (0, 0)),
                pl.BlockSpec((ROWS, COLS), lambda y, x: (0, 0)),
                pl.BlockSpec(
                    (SIDE, 2, COLS, PANEL_DEV),
                    lambda y, x: (lax.rem(y + x[0], SIDE), 0, 0, 0),
                ),
            ],
            out_specs=pl.BlockSpec((SIDE, ROWS, PANEL_DEV), lambda y, x: (y, 0, 0)),
        ),
        out_shape=jax.ShapeDtypeStruct((N_COL, ROWS, PANEL_DEV), bf16),
        compiler_params=params(),
        cost_estimate=pl.CostEstimate(
            flops=4 * ROWS * COLS * N_COL * PANEL_DEV, bytes_accessed=20 << 20, transcendentals=0
        ),
        name="panel",
    )(turn.reshape(1), eta_pairs, gamma_pairs, whole)
    return lax.psum_scatter(
        sums.reshape(N_COL * ROWS, PANEL_DEV), "col", scatter_dimension=0, tiled=True
    )


def exchange(tiles):
    return lax.all_to_all(tiles, ("col", "row"), split_axis=0, concat_axis=0, tiled=True)


def updates(
    eta_pairs,
    gamma_pairs,
    pieces,
    gamma_recoupled,
    ph_factor,
    tile_source,
    tile_owner,
    tile_place,
    sixj_weight,
    live_count,
):
    weights = sixj_weight.astype(f32)
    slots = BLOCKS * CAP
    groups = BLOCKS // GROUP
    rows = CAP * TILE
    dma = pltpu.SemaphoreType.DMA
    held = pltpu.VMEM((BLOCKS, rows, TILE), bf16)
    sent, tiles, factors = pl.pallas_call(
        send_kernel,
        in_specs=[smem_spec()] * 5 + [any_spec()],
        out_specs=[any_spec(), smem_spec(), smem_spec()],
        out_shape=[
            jax.ShapeDtypeStruct((BLOCKS, rows + CODE_ROWS, TILE), bf16),
            jax.ShapeDtypeStruct((slots,), jnp.int32),
            jax.ShapeDtypeStruct((slots,), f32),
        ],
        scratch_shapes=[
            pltpu.SMEM((slots,), jnp.int32),
            pltpu.SMEM((BLOCKS,), jnp.int32),
            pltpu.VMEM((BLOCKS, rows + CODE_ROWS, TILE), bf16),
            pltpu.VMEM((ROWS, COLS), bf16),
            dma((groups,)),
            dma,
        ],
        compiler_params=params(),
        cost_estimate=pl.CostEstimate(flops=0, bytes_accessed=11 << 20, transcendentals=0),
        name="send",
    )(live_count, tile_source, tile_owner, tile_place, weights, eta_pairs)
    sent, pieces = lax.optimization_barrier((sent, pieces))
    panel_sums = panel_part(eta_pairs, gamma_pairs, pieces)
    received = exchange(sent)
    whole = (PH_STATES, PH_STATES)
    answers = pl.pallas_call(
        channel_kernel,
        in_specs=[any_spec(), any_spec(), vmem_spec()],
        out_specs=any_spec(),
        out_shape=jax.ShapeDtypeStruct((BLOCKS, rows, TILE), bf16),
        scratch_shapes=[
            held,
            pltpu.VMEM(whole, bf16),
            pltpu.VMEM(whole, f32),
            pltpu.VMEM(whole, bf16),
            pltpu.VMEM(whole, bf16),
            pltpu.VMEM((BLOCKS, CODE_ROWS, TILE), bf16),
            pltpu.VMEM((BLOCKS, TILE), jnp.int32),
            pltpu.SMEM((BLOCKS, TILE), jnp.int32),
            dma((groups,)),
            dma,
            dma((groups,)),
            dma,
        ],
        compiler_params=params(),
        cost_estimate=pl.CostEstimate(
            flops=4 * PH_STATES**3, bytes_accessed=22 << 20, transcendentals=0
        ),
        name="channel",
    )(received, gamma_recoupled[0], ph_factor.reshape(PH_STATES, 1))
    returned = exchange(answers)
    recoupled_update = pl.pallas_call(
        update_kernel,
        in_specs=[smem_spec(), smem_spec(), any_spec()],
        out_specs=vmem_spec(),
        out_shape=jax.ShapeDtypeStruct((ROWS, COLS), bf16),
        scratch_shapes=[
            held,
            pltpu.VMEM((ROWS, COLS), f32),
            pltpu.SMEM((slots + 8,), jnp.int32),
            dma((groups,)),
        ],
        compiler_params=params(),
        cost_estimate=pl.CostEstimate(flops=0, bytes_accessed=11 << 20, transcendentals=0),
        name="update",
    )(tiles, factors, returned)
    panel_update = pl.pallas_call(
        turn_kernel,
        in_specs=[vmem_spec()],
        out_specs=vmem_spec(),
        out_shape=jax.ShapeDtypeStruct((PANEL_DEV, ROWS), bf16),
        compiler_params=params(),
        name="turn",
    )(panel_sums)
    return (panel_update, recoupled_update)


def local(
    eta_pairs,
    gamma_pairs,
    pair_first,
    pair_second,
    occupancy,
    gamma_recoupled,
    ph_factor,
    tile_source,
    tile_owner,
    tile_place,
    sixj_weight,
    live_count,
):
    pieces = panel_pieces(eta_pairs, gamma_pairs, pair_first, pair_second, occupancy)
    return updates(
        eta_pairs,
        gamma_pairs,
        pieces,
        gamma_recoupled,
        ph_factor,
        tile_source,
        tile_owner,
        tile_place,
        sixj_weight,
        live_count,
    )


def solution(mesh):
    in_specs = (
        P("row", "col"),
        P("row", "col"),
        P("row"),
        P("row"),
        P(),
        P(("row", "col"), None, None),
        P(("row", "col"), None),
        P(("row", "col"), None),
        P(("row", "col"), None),
        P(("row", "col"), None),
        P(("row", "col"), None),
        P(("row", "col")),
    )
    out_specs = (P("col", "row"), P("row", "col"))
    return jax.shard_map(local, mesh=mesh, in_specs=in_specs, out_specs=out_specs, check_vma=False)
```

```python
import jax
import jax.numpy as jnp
from jax import lax
from jax.experimental import pallas as pl
from jax.experimental.pallas import tpu as pltpu
from jax.sharding import PartitionSpec as P

TILE = 128
ORBITS = 240
PH_STATES = 1536
PH_TILES = 12
PANEL_DEV = 128
ROWS = 1536
COLS = 768
COL_TILES = 6
TILES_BLOCK = 72
SLOTS = 144
BLOCKS = 128
CAP = 2
N_ROW = 8
N_COL = 16
SIDE = 4
GROUP = 16
CODE_ROWS = 8
VMEM_LIMIT = 60 * 1024 * 1024

f32 = jnp.float32
bf16 = jnp.bfloat16
SMEM = pltpu.MemorySpace.SMEM
VMEM = pltpu.MemorySpace.VMEM


def smem_spec():
    return pl.BlockSpec(memory_space=SMEM)


def any_spec():
    return pl.BlockSpec(memory_space=pl.ANY)


def vmem_spec():
    return pl.BlockSpec(memory_space=VMEM)


def params():
    return pltpu.CompilerParams(vmem_limit_bytes=VMEM_LIMIT)


def aligned(start, size):
    return pl.ds(pl.multiple_of(start * size, size), size)


def step_through(count, unroll, body):
    def step(i, carry):
        for j in range(unroll):
            body(i * unroll + j)
        return carry

    lax.fori_loop(0, count // unroll, step, 0)


def send_kernel(
    live_ref,
    source_ref,
    owner_ref,
    place_ref,
    weight_ref,
    eta_hbm,
    out_ref,
    tile_ref,
    factor_ref,
    place_of,
    counts,
    held,
    eta_ref,
    sems,
    eta_sem,
):
    eta_copy = pltpu.make_async_copy(eta_hbm, eta_ref, eta_sem)
    eta_copy.start()

    def clear(n):
        tile_ref[n] = 0
        factor_ref[n] = 0.0
        place_of[n] = 0

    step_through(BLOCKS * CAP, 8, clear)

    def clear_count(q):
        counts[q] = 0

    step_through(BLOCKS, 8, clear_count)

    def slot(s, carry):
        owner = owner_ref[0, s]
        q = (owner & (N_COL - 1)) * N_ROW + owner // N_COL
        k = counts[q]
        counts[q] = k + 1
        n = q * CAP + k
        t = source_ref[0, s]
        r = t // COL_TILES
        tile_ref[n] = r * 8 + (t - r * COL_TILES)
        factor_ref[n] = weight_ref[0, s]
        u = place_ref[0, s]
        v = u // PH_TILES
        place_of[n] = v * 16 + (u - v * PH_TILES)
        return carry

    lax.fori_loop(0, live_ref[0], slot, 0)
    lane = lax.broadcasted_iota(jnp.int32, (CODE_ROWS, TILE), 1)
    eta_copy.wait()

    def copy(j):
        part = pl.ds(j * GROUP, GROUP)
        return pltpu.make_async_copy(held.at[part], out_ref.at[part], sems.at[j])

    def group(j, carry):
        def owner(i):
            q = j * GROUP + i
            for k in range(CAP):
                n = q * CAP + k
                t = tile_ref[n]
                tile = eta_ref[aligned(t >> 3, TILE), aligned(t & 7, TILE)]
                held[q, k * TILE : (k + 1) * TILE, :] = (
                    factor_ref[n] * tile.astype(f32)
                ).astype(bf16)
            codes = jnp.where(lane == 0, place_of[q * CAP], place_of[q * CAP + 1])
            held[q, CAP * TILE : CAP * TILE + CODE_ROWS, :] = codes.astype(f32).astype(bf16)

        step_through(GROUP, 4, owner)
        copy(j).start()
        return carry

    lax.fori_loop(0, BLOCKS // GROUP, group, 0)

    def finish(j):
        copy(j).wait()

    step_through(BLOCKS // GROUP, 1, finish)


def turn_kernel(in_ref, out_ref):
    out_ref[...] = in_ref[...].astype(f32).T.astype(bf16)


def update_kernel(
    tile_ref, factor_ref, back_ref, out_ref, held, total, used, sems
):
    def copy(j):
        part = pl.ds(j * GROUP, GROUP)
        return pltpu.make_async_copy(back_ref.at[part], held.at[part], sems.at[j])

    def begin(j):
        copy(j).start()

    step_through(BLOCKS // GROUP, 1, begin)

    def note(i, count):
        for j in range(8):
            n = i * 8 + j
            used[count] = n
            count = count + (factor_ref[n] != 0.0).astype(jnp.int32)
        return count

    count = lax.fori_loop(0, BLOCKS * CAP // 8, note, 0)

    def clear(r):
        total[aligned(r, TILE), :] = jnp.zeros((TILE, COLS), f32)

    step_through(ROWS // TILE, 1, clear)

    def arrive(j, carry):
        copy(j).wait()
        return carry

    batch = 8

    def add(i, arrived):
        last = used[jnp.minimum(i * batch + batch, count) - 1]
        needed = last // (GROUP * CAP) + 1
        lax.fori_loop(arrived, needed, arrive, 0)
        for j in range(batch):
            e = i * batch + j
            n = jnp.where(e < count, used[e], 0)
            factor = jnp.where(e < count, factor_ref[n], 0.0)
            t = tile_ref[n]
            rows, cols = aligned(t >> 3, TILE), aligned(t & 7, TILE)
            at = pl.ds(pl.multiple_of((n & 1) * TILE, TILE), TILE)
            total[rows, cols] += factor * held[n >> 1, at, :].astype(f32)
        return jnp.maximum(arrived, needed)

    arrived = lax.fori_loop(0, (count + batch - 1) // batch, add, 0)
    lax.fori_loop(arrived, BLOCKS // GROUP, arrive, 0)

    def finish(r):
        rows = aligned(r, TILE)
        out_ref[rows, :] = total[rows, :].astype(bf16)

    step_through(ROWS // TILE, 1, finish)


def channel_kernel(
    got_ref,
    gamma_hbm,
    scale_ref,
    out_ref,
    held,
    gamma_ref,
    total,
    eta,
    product,
    code_rows,
    codes,
    place_ref,
    got_sems,
    gamma_sem,
    out_sems,
    code_sem,
):
    code_copy = pltpu.make_async_copy(
        got_ref.at[:, pl.ds(CAP * TILE, CODE_ROWS)], code_rows, code_sem
    )
    code_copy.start()

    def copy(j):
        part = pl.ds(j * GROUP, GROUP)
        return pltpu.make_async_copy(
            got_ref.at[part, pl.ds(0, CAP * TILE)], held.at[part], got_sems.at[j]
        )

    gamma_copy = pltpu.make_async_copy(gamma_hbm, gamma_ref, gamma_sem)

    def begin(j):
        copy(j).start()

    step_through(BLOCKS // GROUP, 1, begin)
    gamma_copy.start()
    code_copy.wait()
    codes[...] = code_rows[:, 0, :].astype(f32).astype(jnp.int32)
    place_copy = pltpu.make_async_copy(codes, place_ref, code_sem)
    place_copy.start()

    def clear(r):
        total[aligned(r, TILE), :] = jnp.zeros((TILE, PH_STATES), f32)

    step_through(PH_TILES, 1, clear)
    place_copy.wait()

    def place(b, k):
        code = place_ref[b, k]
        return aligned(code >> 4, TILE), aligned(code & 15, TILE)

    def group(j, carry):
        copy(j).wait()

        def block(i):
            b = j * GROUP + i
            for k in range(CAP):
                rows, cols = place(b, k)
                total[rows, cols] += held[b, k * TILE : (k + 1) * TILE, :].astype(f32)

        step_through(GROUP, 4, block)
        return carry

    lax.fori_loop(0, BLOCKS // GROUP, group, 0)

    def settle(r):
        rows = aligned(r, TILE)
        eta[rows, :] = total[rows, :].astype(bf16)

    step_through(PH_TILES, 1, settle)
    gamma_copy.wait()
    width = 768

    def multiply(c):
        cols = aligned(c, width)
        scale = scale_ref[...]
        gamma_scaled = (scale * gamma_ref[:, cols].astype(f32)).astype(bf16)
        eta_scaled = (-scale * eta[:, cols].astype(f32)).astype(bf16)
        for h in range(2):
            rows = pl.ds(h * width, width)
            part = jnp.dot(eta[rows, :], gamma_scaled, preferred_element_type=f32)
            part += jnp.dot(gamma_ref[rows, :], eta_scaled, preferred_element_type=f32)
            product[rows, cols] = part.astype(bf16)

    step_through(PH_STATES // width, 1, multiply)

    def back(j):
        part = pl.ds(j * GROUP, GROUP)
        return pltpu.make_async_copy(held.at[part], out_ref.at[part], out_sems.at[j])

    def answers(j, carry):
        def block(i):
            b = j * GROUP + i
            for k in range(CAP):
                rows, cols = place(b, k)
                held[b, k * TILE : (k + 1) * TILE, :] = product[rows, cols]

        step_through(GROUP, 4, block)
        back(j).start()
        return carry

    lax.fori_loop(0, BLOCKS // GROUP, answers, 0)

    def finish(j):
        back(j).wait()

    step_through(BLOCKS // GROUP, 1, finish)


def panel_kernel(x_ref, eta_ref, gamma_ref, panel_ref, out_ref):
    gamma_cols = jnp.concatenate([panel_ref[k, 0] for k in range(SIDE)], axis=1)
    eta_cols = jnp.concatenate([panel_ref[k, 1] for k in range(SIDE)], axis=1)
    part = jnp.dot(eta_ref[...], gamma_cols, preferred_element_type=f32)
    part -= jnp.dot(gamma_ref[...], eta_cols, preferred_element_type=f32)
    part = part.astype(bf16)
    for k in range(SIDE):
        out_ref[k] = part[:, k * PANEL_DEV : (k + 1) * PANEL_DEV]


def orbit_lookup(pair_ids, occupancy):
    orbit_ids = jnp.arange(occupancy.shape[0], dtype=jnp.int32)
    return jnp.sum(
        jnp.where(pair_ids[:, None] == orbit_ids[None, :], occupancy[None, :], 0.0), axis=1
    )


def panel_pieces(eta_pairs, gamma_pairs, pair_first, pair_second, occupancy):
    factor = 1.0 - orbit_lookup(pair_first, occupancy) - orbit_lookup(pair_second, occupancy)

    def weigh(pairs):
        return (factor[:, None] * pairs[:, :PANEL_DEV].astype(f32)).astype(bf16)

    halves = jnp.stack([weigh(gamma_pairs), weigh(eta_pairs)]).reshape(2, 2, COLS, PANEL_DEV)
    odd = lax.axis_index("col") % 2 == 1

    def swap(first, second):
        return jnp.where(odd, second, first), jnp.where(odd, first, second)

    def target(i, c, h):
        x = (i // 2 + c // SIDE + i % 2 + 2 * h) % SIDE
        return (2 * x + c % SIDE // 2) * N_COL + 2 * i + h

    def route(flip):
        return [
            (i * N_COL + c, target(i, c, (c + flip) % 2))
            for i in range(N_ROW)
            for c in range(N_COL)
        ]

    same, other = swap(halves[:, 0], halves[:, 1])
    same = lax.ppermute(same, ("row", "col"), route(0))
    other = lax.ppermute(other, ("row", "col"), route(1))
    return jnp.stack(swap(same, other))


def panel_part(eta_pairs, gamma_pairs, pieces):
    whole = lax.all_gather(
        pieces.reshape(4 * COLS, PANEL_DEV), "row", axis=0, tiled=True
    ).reshape(N_COL, 2, COLS, PANEL_DEV)
    me = lax.axis_index("col")
    turn = me // SIDE + me // 2 % 2 + me % 2 * 2
    sums = pl.pallas_call(
        panel_kernel,
        grid_spec=pltpu.PrefetchScalarGridSpec(
            num_scalar_prefetch=1,
            grid=(2, SIDE),
            in_specs=[
                pl.BlockSpec((ROWS // 2, COLS), lambda r, y, x: (r, 0)),
                pl.BlockSpec((ROWS // 2, COLS), lambda r, y, x: (r, 0)),
                pl.BlockSpec(
                    (SIDE, 2, COLS, PANEL_DEV),
                    lambda r, y, x: (lax.rem(y + x[0], SIDE), 0, 0, 0),
                ),
            ],
            out_specs=pl.BlockSpec((SIDE, ROWS // 2, PANEL_DEV), lambda r, y, x: (y, r, 0)),
        ),
        out_shape=jax.ShapeDtypeStruct((N_COL, ROWS, PANEL_DEV), bf16),
        compiler_params=params(),
        cost_estimate=pl.CostEstimate(
            flops=4 * ROWS * COLS * N_COL * PANEL_DEV, bytes_accessed=20 << 20, transcendentals=0
        ),
        name="panel",
    )(turn.reshape(1), eta_pairs, gamma_pairs, whole)
    return lax.psum_scatter(
        sums.reshape(N_COL * ROWS, PANEL_DEV), "col", scatter_dimension=0, tiled=True
    )


def exchange(tiles):
    return lax.all_to_all(tiles, ("col", "row"), split_axis=0, concat_axis=0, tiled=True)


def updates(
    eta_pairs,
    gamma_pairs,
    pieces,
    gamma_recoupled,
    ph_factor,
    tile_source,
    tile_owner,
    tile_place,
    sixj_weight,
    live_count,
):
    weights = sixj_weight.astype(f32)
    slots = BLOCKS * CAP
    groups = BLOCKS // GROUP
    rows = CAP * TILE
    dma = pltpu.SemaphoreType.DMA
    held = pltpu.VMEM((BLOCKS, rows, TILE), bf16)
    sent, tiles, factors = pl.pallas_call(
        send_kernel,
        in_specs=[smem_spec()] * 5 + [any_spec()],
        out_specs=[any_spec(), smem_spec(), smem_spec()],
        out_shape=[
            jax.ShapeDtypeStruct((BLOCKS, rows + CODE_ROWS, TILE), bf16),
            jax.ShapeDtypeStruct((slots,), jnp.int32),
            jax.ShapeDtypeStruct((slots,), f32),
        ],
        scratch_shapes=[
            pltpu.SMEM((slots,), jnp.int32),
            pltpu.SMEM((BLOCKS,), jnp.int32),
            pltpu.VMEM((BLOCKS, rows + CODE_ROWS, TILE), bf16),
            pltpu.VMEM((ROWS, COLS), bf16),
            dma((groups,)),
            dma,
        ],
        compiler_params=params(),
        cost_estimate=pl.CostEstimate(flops=0, bytes_accessed=11 << 20, transcendentals=0),
        name="send",
    )(live_count, tile_source, tile_owner, tile_place, weights, eta_pairs)
    sent, pieces = lax.optimization_barrier((sent, pieces))
    panel_sums = panel_part(eta_pairs, gamma_pairs, pieces)
    received = exchange(sent)
    whole = (PH_STATES, PH_STATES)
    answers = pl.pallas_call(
        channel_kernel,
        in_specs=[any_spec(), any_spec(), vmem_spec()],
        out_specs=any_spec(),
        out_shape=jax.ShapeDtypeStruct((BLOCKS, rows, TILE), bf16),
        scratch_shapes=[
            held,
            pltpu.VMEM(whole, bf16),
            pltpu.VMEM(whole, f32),
            pltpu.VMEM(whole, bf16),
            pltpu.VMEM(whole, bf16),
            pltpu.VMEM((BLOCKS, CODE_ROWS, TILE), bf16),
            pltpu.VMEM((BLOCKS, TILE), jnp.int32),
            pltpu.SMEM((BLOCKS, TILE), jnp.int32),
            dma((groups,)),
            dma,
            dma((groups,)),
            dma,
        ],
        compiler_params=params(),
        cost_estimate=pl.CostEstimate(
            flops=4 * PH_STATES**3, bytes_accessed=22 << 20, transcendentals=0
        ),
        name="channel",
    )(received, gamma_recoupled[0], ph_factor.reshape(PH_STATES, 1))
    returned = exchange(answers)
    recoupled_update = pl.pallas_call(
        update_kernel,
        in_specs=[smem_spec(), smem_spec(), any_spec()],
        out_specs=vmem_spec(),
        out_shape=jax.ShapeDtypeStruct((ROWS, COLS), bf16),
        scratch_shapes=[
            held,
            pltpu.VMEM((ROWS, COLS), f32),
            pltpu.SMEM((slots + 8,), jnp.int32),
            dma((groups,)),
        ],
        compiler_params=params(),
        cost_estimate=pl.CostEstimate(flops=0, bytes_accessed=11 << 20, transcendentals=0),
        name="update",
    )(tiles, factors, returned)
    panel_update = pl.pallas_call(
        turn_kernel,
        in_specs=[vmem_spec()],
        out_specs=vmem_spec(),
        out_shape=jax.ShapeDtypeStruct((PANEL_DEV, ROWS), bf16),
        compiler_params=params(),
        name="turn",
    )(panel_sums)
    return (panel_update, recoupled_update)


def local(
    eta_pairs,
    gamma_pairs,
    pair_first,
    pair_second,
    occupancy,
    gamma_recoupled,
    ph_factor,
    tile_source,
    tile_owner,
    tile_place,
    sixj_weight,
    live_count,
):
    pieces = panel_pieces(eta_pairs, gamma_pairs, pair_first, pair_second, occupancy)
    return updates(
        eta_pairs,
        gamma_pairs,
        pieces,
        gamma_recoupled,
        ph_factor,
        tile_source,
        tile_owner,
        tile_place,
        sixj_weight,
        live_count,
    )


def solution(mesh):
    in_specs = (
        P("row", "col"),
        P("row", "col"),
        P("row"),
        P("row"),
        P(),
        P(("row", "col"), None, None),
        P(("row", "col"), None),
        P(("row", "col"), None),
        P(("row", "col"), None),
        P(("row", "col"), None),
        P(("row", "col"), None),
        P(("row", "col")),
    )
    out_specs = (P("col", "row"), P("row", "col"))
    return jax.shard_map(local, mesh=mesh, in_specs=in_specs, out_specs=out_specs, check_vma=False)
```
